32 devices in a mesh: wide: 16 (over z, y, x), narrow: 2 (over core).
Axes of the slice: x: 2, y: 2, z: 4, core: 2. Of those that a mesh axis runs over, the one named last changes fastest.
Arguments:
- tokens: bfloat16 [1024, 2048], P('wide'), may hold values from -6 to 6
- routes: int32 [1024, 6], P('wide'), may hold values from 0 to 15, all different within a row; in each aligned block of 64 rows (0 to 63, 64 to 127, ...) at most 44 rows name the same one
- route_weight: float32 [1024, 6], P('wide'), may hold values from 0.1 to 0.8
- w_gate: bfloat16 [16, 1408, 2048], P('wide', None, 'narrow'), may hold values from -0.1875 to 0.1875
- w_up: bfloat16 [16, 1408, 2048], P('wide', None, 'narrow'), may hold values from -0.1875 to 0.1875
- w_down: bfloat16 [16, 1408, 2048], P('wide', None, 'narrow'), may hold values from -0.15625 to 0.15625
Outputs:
- combined: bfloat16 [1024, 2048], P('wide', 'narrow')
The draws below stay inside these ranges and needn't reach their ends.
Inputs may be any that keep to these rules, and one draw needn't show every extreme that they name: `routes`: each row names 6 different experts. Within each aligned block of 64 rows no expert is named by more than 44 rows, and in some block an expert is named by exactly 44 rows.
All inputs are finite; a program needn't handle non-finite values.
Results may differ from the reference program's by a relative error of at most 0.029.
Values may be sent and summed in bfloat16 or wider, within the bound.
A program may use at most 64 MiB of HBM per device.

```python
import math
import jax
import jax.numpy as jnp
import numpy as np
from jax import lax

D = 2048
FF = 1408
TOP = 6
TOK_DEV = 64
EXPERTS = 16
TOKENS = 1024
CAP = 44
N_WIDE = 16
N_NARROW = 2


def raised(result, rng, source, target, shards_of, factor):
    owner, partner = [(jnp.arange(result.shape[axis_at]) // (result.shape[axis_at] // shards_of)).reshape([-1 if axis == axis_at else 1 for axis in range(result.ndim)]) for axis_at in (source, target)]
    chosen = jax.random.permutation(rng, shards_of)[partner]
    strong = (owner == chosen) | (owner == (partner + shards_of // 2) % shards_of)
    return jnp.where(strong, factor * result, result)


def block_scale(key, dims, split, smallest, top_value):
    loudness = 1.0
    for dim, blocks in split:
        steps = jax.random.uniform(jax.random.fold_in(jax.random.fold_in(key, 6), dim), (blocks,), jnp.float32, smallest / len(split), top_value / len(split))
        loudness = loudness * jnp.repeat(jnp.exp(steps), dims[dim] // blocks).reshape((-1,) + (1,) * (len(dims) - 1 - dim))
    return loudness


def routed_block(own_key, own, number, rows, count, top, limit, slope):
    ranking = jax.random.permutation(own_key, count)
    packed, ordinary = shares(count, rows * top, limit, slope, True), shares(count, rows * top, limit, slope, False)
    places = jnp.arange(count)

    def named(lengths, turn):
        used = int((lengths > 0).sum())
        fixed = max(1, used // 4)
        passed = fixed + (places - fixed + turn * (used - fixed)) % max(1, count - fixed)
        return jnp.zeros((count,), jnp.int32).at[ranking[jnp.where(places < fixed, places, passed)]].set(jnp.asarray(lengths, jnp.int32))

    lengths = jnp.where(number % 4 == 0, named(packed, number // 4), named(ordinary, number - number // 4 - 1))
    mixed = jax.random.permutation(jax.random.fold_in(own, 3), count)
    source_of, taker = mixed[0:count // 2 * 2:2], mixed[1:count // 2 * 2:2]
    margin = jnp.minimum(lengths[source_of] - 1, limit - lengths[taker]) // 2
    margin = jnp.where((source_of == ranking[0]) | (taker == ranking[0]) | (lengths[taker] == 0), 0, jnp.maximum(margin, 0))
    passed = jax.random.randint(jax.random.fold_in(own, 4), (count // 2,), 0, 1 << 20) % (margin + 1)
    lengths = lengths.at[source_of].add(-passed).at[taker].add(passed)
    members = jnp.searchsorted(jnp.cumsum(lengths), jnp.arange(rows * top), side="right").astype(jnp.int32)
    grid = members.reshape(top, rows).T
    grid = grid[jax.random.permutation(jax.random.fold_in(own, 1), rows)]
    turn = jax.random.randint(jax.random.fold_in(own, 2), (rows, 1), 0, top)
    return jnp.take_along_axis(grid, (jnp.arange(top)[None, :] + turn) % top, axis=1)


def shares(number_of, total, reach, slope, full):
    loads = [(1 << 20) // math.isqrt(grade ** slope) + 1 for grade in range(1, number_of + 1)]
    largest = reach if full else min(reach, max(-(-total // number_of), total * loads[0] // sum(loads)))
    least = 1 if total - largest >= number_of - 1 else 0
    holding, surplus = [largest] + [least] * (number_of - 1), total - largest - least * (number_of - 1)
    while surplus > 0:
        free = [i for i in range(1, number_of) if holding[i] < largest] or [i for i in range(1, number_of) if holding[i] < reach]
        mass, remaining = sum([loads[i] for i in free]), surplus
        for i in free:
            addition = min(reach - holding[i], max(1, remaining * loads[i] // mass), surplus)
            holding[i] = holding[i] + addition
            surplus = surplus - addition
    return np.array(holding)


def normal_values(rng, dims, spread, bound, shards=(), held_as=jnp.bfloat16):
    array = jax.random.normal(rng, dims, jnp.float32) * spread
    if len(shards) > 0:
        array = block_scale(rng, dims, shards, -0.22, 0.18) * array
    return jnp.clip(array, min=-bound, max=bound).astype(held_as)


def bell_draw_with(stream_key, shape, deviation, reach, split, heavy, held_as=jnp.bfloat16):
    array = deviation * jax.random.normal(stream_key, shape, jnp.float32)
    if split:
        array = array * block_scale(stream_key, shape, split, -0.22, 0.18)
    return jnp.clip(raised(array, jax.random.fold_in(stream_key, 3), *heavy), -reach, reach).astype(held_as)


def setup_inputs(seed: int = 0) -> dict:
    keys = jax.random.split(jax.random.key(seed), 7)
    tokens = normal_values(keys[0], (TOKENS, D), 1.0, 6.0, ((0, 16),))
    routes_keys = jax.random.split(jax.random.fold_in(keys[1], 1), TOKENS // TOK_DEV)
    routes_turns = jax.random.permutation(jax.random.fold_in(keys[1], 3), TOKENS // TOK_DEV)
    routes = jax.vmap(lambda own, number: routed_block(jax.random.fold_in(keys[1], 2), own, number, TOK_DEV, EXPERTS, TOP, CAP, 2))(routes_keys, routes_turns).reshape((TOKENS, TOP))
    route_weight = jnp.clip(0.1 + 0.7 * jax.random.uniform(keys[2], (TOKENS, TOP), jnp.float32) ** block_scale(keys[2], (TOKENS, TOP), ((0, 16),), -0.2, 0.2), 0.1, 0.8)
    w_gate = bell_draw_with(keys[3], (EXPERTS, FF, D), D ** -0.5, 0.1875, ((0, 16), (2, 2)), (2, 1, 2, 2.0))
    w_up = bell_draw_with(keys[4], (EXPERTS, FF, D), D ** -0.5, 0.1875, ((0, 16), (2, 2)), (2, 1, 2, 2.0))
    w_down = normal_values(keys[5], (EXPERTS, FF, D), FF ** -0.5, 0.15625, ((0, 16), (2, 2)))
    return {"tokens": tokens, "routes": routes, "route_weight": route_weight, "w_gate": w_gate, "w_up": w_up, "w_down": w_down}


def slots_of(route_block):
    flat_routes = route_block.reshape(-1)
    onehot = (flat_routes[:, None] == jnp.arange(EXPERTS, dtype=jnp.int32)[None, :]).astype(jnp.int32)
    before = jnp.cumsum(onehot, 0) - onehot
    return jnp.sum(before * onehot, 1).reshape(route_block.shape).astype(jnp.int32)


def block_sums(rows_blocks, matrix, column_width):
    blocks = matrix.reshape(FF, N_NARROW, column_width).astype(jnp.float32)
    parts = jnp.einsum('snc,fnc->nsf', rows_blocks, blocks)
    parts = lax.optimization_barrier(parts.astype(jnp.bfloat16)).astype(jnp.float32)
    return jnp.sum(parts, 0)


def reference(tokens, routes, route_weight, w_gate, w_up, w_down):
    slot_count = N_WIDE * CAP
    column_width = D // N_NARROW
    route_blocks = routes.reshape(N_WIDE, TOK_DEV, TOP)
    slot = jax.vmap(slots_of)(route_blocks).reshape(TOKENS, TOP)
    source_block = (jnp.arange(TOKENS, dtype=jnp.int32) // TOK_DEV)[:, None]
    place = (routes * slot_count + source_block * CAP + slot).astype(jnp.int32)
    owner = jnp.broadcast_to(jnp.arange(TOKENS, dtype=jnp.int32)[:, None], (TOKENS, TOP))
    table = jnp.full((EXPERTS * slot_count,), TOKENS, dtype=jnp.int32)
    table = table.at[place.reshape(-1)].set(owner.reshape(-1)).reshape(EXPERTS, slot_count)
    padded = jnp.concatenate([tokens, jnp.zeros((1, D), tokens.dtype)], 0)

    def one_expert(inputs):
        row_index, gate_matrix, up_matrix, down_matrix = inputs
        rows = padded[row_index]
        rows_blocks = rows.reshape(slot_count, N_NARROW, column_width).astype(jnp.float32)
        gate = block_sums(rows_blocks, gate_matrix, column_width)
        up = block_sums(rows_blocks, up_matrix, column_width)
        hidden = (jax.nn.silu(gate) * up).astype(jnp.bfloat16)
        return jnp.dot(hidden, down_matrix, preferred_element_type=jnp.float32).astype(jnp.bfloat16)

    expert_out = lax.map(one_expert, (table, w_gate, w_up, w_down))
    flat_rows = expert_out.reshape(EXPERTS * slot_count, D)
    picked = flat_rows[place].astype(jnp.float32)
    combined = jnp.sum(route_weight[:, :, None] * picked, 1)
    return combined.astype(jnp.bfloat16)
```

```python
import functools

import jax
import jax.numpy as jnp
from jax import lax
from jax.experimental import pallas as pl
from jax.experimental.pallas import tpu as pltpu
from jax.sharding import PartitionSpec as P


def slot_numbers(routes, experts):
    flat_routes = routes.reshape(-1)
    onehot = (flat_routes[:, None] == jnp.arange(experts, dtype=jnp.int32)[None, :]).astype(
        jnp.int32
    )
    before = jnp.cumsum(onehot, 0) - onehot
    return jnp.sum(before * onehot, 1).reshape(routes.shape)


def slots_plan(tokens, routes, route_weight, w_gate, w_up, w_down):
    tok_count = tokens.shape[0]
    model_width = tokens.shape[1]
    wide_count = lax.axis_size("wide")
    narrow_count = lax.axis_size("narrow")
    local_experts = w_gate.shape[0]
    experts = local_experts * wide_count
    capacity = max(2, (11 * tok_count + experts - 1) // experts)
    column_width = model_width // narrow_count
    slot_index = slot_numbers(routes, experts)
    target = routes * capacity + slot_index
    lane_ids = jnp.arange(experts * capacity, dtype=jnp.int32)
    picker = jnp.sum((lane_ids[:, None, None] == target[None, :, :]).astype(jnp.int32), 2).astype(
        jnp.bfloat16
    )
    columns = lax.dynamic_slice_in_dim(
        tokens, lax.axis_index("narrow") * column_width, column_width, 1
    )
    outgoing = jnp.dot(picker, columns, preferred_element_type=jnp.float32).astype(jnp.bfloat16)
    outgoing = outgoing.reshape(experts, capacity, column_width)
    received = lax.all_to_all(outgoing, "wide", split_axis=0, concat_axis=1, tiled=True)
    expert_rows = received[0]
    slot_total = expert_rows.shape[0]
    gate_matrix = w_gate[0]
    up_matrix = w_up[0]
    down_matrix = w_down[0]
    gate_term = jnp.einsum(
        "sc,fc->fs", expert_rows, gate_matrix, preferred_element_type=jnp.float32
    )
    up_term = jnp.einsum("sc,fc->fs", expert_rows, up_matrix, preferred_element_type=jnp.float32)
    sums = lax.psum_scatter(
        jnp.concatenate([gate_term, up_term], 1).astype(jnp.bfloat16),
        "narrow",
        scatter_dimension=0,
        tiled=True,
    ).astype(jnp.float32)
    hidden = (jax.nn.silu(sums[:, :slot_total]) * sums[:, slot_total:]).astype(jnp.bfloat16)
    produced = jnp.einsum(
        "fs,fc->sc",
        lax.all_gather(hidden, "narrow", axis=0, tiled=True),
        down_matrix,
        preferred_element_type=jnp.float32,
    )
    expert_out = produced.astype(jnp.bfloat16).reshape(local_experts, slot_total, column_width)
    returned = lax.all_to_all(expert_out, "wide", split_axis=1, concat_axis=0, tiled=True)
    flat_rows = returned.reshape(experts * capacity, column_width)
    picked = jnp.take(flat_rows, target, axis=0).astype(jnp.float32)
    combined = jnp.sum(picked * route_weight[:, :, None], 1)
    return combined.astype(jnp.bfloat16)


WAVES = 2
NT = (((1,), (1,)), ((), ()))
NN = (((1,), (0,)), ((), ()))


def place(column, z):
    return (z // 2) * 8 + column * 2 + z % 2


def kernel(
    tokens, routes, weights, gate_hbm, up_hbm, down_hbm, out,
    tok, gate_up, down, coef, scale, gsend, grecv, hid, part, back, zsend, zrecv,
    load_sem, own_sem, ag_send, ag_recv, cf_send, cf_recv,
    g_send, g_recv, h_send, h_recv, rs_send, rs_recv, z_send, z_recv,
):
    w = lax.axis_index("wide")
    n = lax.axis_index("narrow")
    z = w // 4
    x_peer = w + 1 - 2 * (w % 2)
    y_peer = w + 2 - 4 * ((w // 2) % 2)
    tiles = gate_up.shape[0]
    rows = tok.shape[2]
    half_rows = 8 * rows
    cols = tok.shape[3]

    def copy(src, dst, send, recv, wide, narrow=n):
        return pltpu.make_async_remote_copy(
            src_ref=src, dst_ref=dst, send_sem=send, recv_sem=recv,
            device_id=(wide, narrow), device_id_type=pl.DeviceIdType.MESH,
        )

    def arrived(dst, recv, wide=x_peer):
        copy(dst, dst, recv, recv, wide).wait_recv()

    sent = []

    def send(src, dst, send_sem, recv_sem, wide, narrow=n):
        c = copy(src, dst, send_sem, recv_sem, wide, narrow)
        c.start()
        sent.append(c)

    def z_peer(k):
        return (w + 4 * k) % 16

    barrier = pltpu.get_barrier_semaphore()
    for wide, narrow in [(z_peer(k), n) for k in (1, 2, 3)] + [(x_peer, n), (y_peer, n), (w, 1 - n)]:
        pl.semaphore_signal(barrier, inc=1, device_id=(wide, narrow), device_id_type=pl.DeviceIdType.MESH)
    loads = [
        pltpu.make_async_copy(gate_hbm, gate_up.at[:, 0], load_sem.at[0]),
        pltpu.make_async_copy(up_hbm, gate_up.at[:, 1], load_sem.at[1]),
        pltpu.make_async_copy(down_hbm, down, load_sem.at[2]),
    ]
    own_block = [tokens.at[pl.ds(v * rows, rows), pl.ds(pl.multiple_of(n * cols, cols), cols)] for v in range(WAVES)]
    own_copy = [
        pltpu.make_async_copy(own_block[v], tok.at[v, place(0, z)], own_sem.at[v]) for v in range(WAVES)
    ]
    pl.semaphore_wait(barrier, 6)

    def send_z(v):
        for k in (1, 3, 2):
            send(own_block[v], tok.at[v, place(0, z)], ag_send.at[v, 0, k], ag_recv.at[v, 0, z], z_peer(k))

    def send_xy(v, src, from_z):
        send(src, tok.at[v, place(1, from_z)], ag_send.at[v, 1, from_z], ag_recv.at[v, 1, from_z], x_peer)
        send(src, tok.at[v, place(2, from_z)], ag_send.at[v, 2, from_z], ag_recv.at[v, 2, from_z], y_peer)

    def pass_column(v):
        for k in (1, 3, 2):
            from_z = (z + k) % 4
            block = tok.at[v, place(0, from_z)]
            arrived(block, ag_recv.at[v, 0, from_z])
            send_xy(v, block, from_z)

    def pass_diagonal(v):
        for low in (0, 1):
            for h in (0, 1):
                from_z = 2 * h + low
                block = tok.at[v, place(1 + h, from_z)]
                arrived(block, ag_recv.at[v, 1 + h, from_z])
                send(
                    block, tok.at[v, place(3, from_z)], ag_send.at[v, 3, from_z], ag_recv.at[v, 3, from_z],
                    y_peer if h == 0 else x_peer,
                )

    def gather_rest(v):
        for low in (0, 1):
            for h in (0, 1):
                from_z = 2 * h + low
                arrived(tok.at[v, place(2 - h, from_z)], ag_recv.at[v, 2 - h, from_z])
                arrived(tok.at[v, place(3, from_z)], ag_recv.at[v, 3, from_z])
        own_copy[v].wait()

    send_z(0)
    send_xy(0, own_block[0], z)
    send_z(1)
    for c in own_copy + loads:
        c.start()

    lane = lax.broadcasted_iota(jnp.int32, (8, 128), 1)
    packed = jnp.zeros((8, 128), jnp.float32)
    for g in range(tokens.shape[0] // 8):
        for k in range(routes.shape[1]):
            chosen = routes[pl.ds(8 * g, 8), k : k + 1] + 16 * g
            packed += jnp.where(lane == chosen, weights[pl.ds(8 * g, 8), k : k + 1], 0.0)
    coef[0, z] = packed
    for k in (1, 2, 3):
        send(coef.at[0, z], coef.at[0, z], cf_send.at[k], cf_recv.at[z], z_peer(k))

    pass_column(0)
    send_xy(1, own_block[1], z)
    pass_diagonal(0)
    pass_column(1)
    for k in (1, 2, 3):
        from_z = (z + k) % 4
        arrived(coef.at[0, from_z], cf_recv.at[from_z])
    send(coef.at[0], coef.at[1], cf_send.at[4], cf_recv.at[4], x_peer)
    send(coef.at[0], coef.at[2], cf_send.at[5], cf_recv.at[5], y_peer)
    for c in loads[:2]:
        c.wait()
    gather_rest(0)

    def tile(i):
        return gate_up[i].reshape(2 * gate_up.shape[2], cols)

    def half(v, h):
        return tok[v, pl.ds(8 * h, 8)].reshape(half_rows, cols)

    def partner_sums(v):
        @pl.loop(0, tiles)
        def _(i):
            sums = lax.dot_general(half(v, 1 - n), tile(i), NT, preferred_element_type=jnp.float32)
            gsend[v, i] = sums.astype(jnp.bfloat16)
            copy(gsend.at[v, i], grecv.at[v, i], g_send.at[v, i], g_recv.at[v, i], w, 1 - n).start()

    def own_hidden(v):
        @pl.loop(0, tiles)
        def _(i):
            sums = lax.dot_general(half(v, n), tile(i), NT, preferred_element_type=jnp.float32)
            arrived(grecv.at[v, i], g_recv.at[v, i])
            sums += grecv[v, i].astype(jnp.float32)
            gate, up = sums[:, :128], sums[:, 128:]
            lanes = pl.ds(pl.multiple_of(i * 128, 128), 128)
            hid[v, n, :, lanes] = (gate / (1.0 + jnp.exp(-gate)) * up).astype(jnp.bfloat16)
            there = hid.at[v, n, :, lanes]
            copy(there, there, h_send.at[v, i], h_recv.at[v, i], w, 1 - n).start()

    def outputs(v, h):
        column = scale[v, pl.ds(8 * h, 8)].reshape(half_rows, 128)[:, 0:1]

        @pl.loop(0, cols // 256)
        def _(i):
            lanes = pl.ds(pl.multiple_of(i * 256, 256), 256)
            acc = lax.dot_general(hid[v, h], down[:, lanes], NN, preferred_element_type=jnp.float32)
            part[v, pl.ds(8 * h, 8), :, lanes] = (acc * column).astype(jnp.bfloat16).reshape(8, rows, 256)

    def other_hidden(v):
        @pl.loop(0, tiles)
        def _(i):
            lanes = pl.ds(pl.multiple_of(i * 128, 128), 128)
            arrived(hid.at[v, 1 - n, :, lanes], h_recv.at[v, i])

    def send_half(v, h):
        peer = x_peer + h * (y_peer - x_peer)
        for low in (0, 1):
            at = 2 * h + low
            send(part.at[v, place(3, at)], back.at[v, 0, at], rs_send.at[v, 0, at], rs_recv.at[v, 0, at], peer)
        for low in (0, 1):
            at = 2 * h + low
            send(
                part.at[v, place(1 + h, at)], back.at[v, 1 + h, at],
                rs_send.at[v, 1 + h, at], rs_recv.at[v, 1 + h, at], peer,
            )

    def relay_sums(v):
        for low in (0, 1):
            for h in (0, 1):
                at = 2 * h + low
                arrived(back.at[v, 0, at], rs_recv.at[v, 0, at])
                mine = part[v, place(2 - h, at)].astype(jnp.float32)
                part[v, place(2 - h, at)] = (mine + back[v, 0, at].astype(jnp.float32)).astype(jnp.bfloat16)
                send(
                    part.at[v, place(2 - h, at)], back.at[v, 2 - h, at],
                    rs_send.at[v, 2 - h, at], rs_recv.at[v, 2 - h, at], y_peer if h == 0 else x_peer,
                )

    def column_sums(v):
        for k in (2, 1, 3, 0):
            at = (z + k) % 4
            arrived(back.at[v, 1, at], rs_recv.at[v, 1, at])
            arrived(back.at[v, 2, at], rs_recv.at[v, 2, at])
            total = part[v, place(0, at)].astype(jnp.float32)
            total += back[v, 1, at].astype(jnp.float32) + back[v, 2, at].astype(jnp.float32)
            if k == 0:
                zrecv[v, z] = total.astype(jnp.bfloat16)
            else:
                zsend[v, k] = total.astype(jnp.bfloat16)
                send(zsend.at[v, k], zrecv.at[v, z], z_send.at[v, k], z_recv.at[v, z], z_peer(k))

    def finish(v):
        for k in (1, 3, 2):
            at = (z + k) % 4
            arrived(zrecv.at[v, at], z_recv.at[v, at])
        total = zrecv[v, 0].astype(jnp.float32) + zrecv[v, 1].astype(jnp.float32)
        total += zrecv[v, 2].astype(jnp.float32) + zrecv[v, 3].astype(jnp.float32)
        out[pl.ds(v * rows, rows), :] = total.astype(jnp.bfloat16)

    partner_sums(0)
    arrived(coef.at[1], cf_recv.at[4])
    send(coef.at[1], coef.at[3], cf_send.at[6], cf_recv.at[6], y_peer)
    own_hidden(0)
    pass_diagonal(1)
    arrived(coef.at[2], cf_recv.at[5])
    arrived(coef.at[3], cf_recv.at[6])
    lane = lax.broadcasted_iota(jnp.int32, (4, 8, 128), 2)
    for column in range(4):
        block = coef[column]
        for g in range(tokens.shape[0] // 8):
            mine = jnp.sum(jnp.where(lane == 16 * g + w, block, 0.0), 2, keepdims=True)
            mine = jnp.broadcast_to(mine, (4, 8, 128))
            for at in range(4):
                scale[g * 8 // rows, place(column, at), g % (rows // 8)] = mine[at]
    loads[2].wait()
    outputs(0, n)
    send_half(0, n)
    other_hidden(0)
    outputs(0, 1 - n)
    send_half(0, 1 - n)

    gather_rest(1)
    partner_sums(1)
    relay_sums(0)
    own_hidden(1)
    column_sums(0)
    outputs(1, n)
    send_half(1, n)
    other_hidden(1)
    outputs(1, 1 - n)
    send_half(1, 1 - n)
    relay_sums(1)
    column_sums(1)
    finish(0)
    finish(1)

    for c in sent:
        c.wait_send()
    for v in range(WAVES):

        @pl.loop(0, tiles)
        def _(i):
            lanes = pl.ds(pl.multiple_of(i * 128, 128), 128)
            there = hid.at[v, n, :, lanes]
            copy(gsend.at[v, i], grecv.at[v, i], g_send.at[v, i], g_recv.at[v, i], w, 1 - n).wait_send()
            copy(there, there, h_send.at[v, i], h_recv.at[v, i], w, 1 - n).wait_send()


def gather_plan(tokens, routes, route_weight, w_gate, w_up, w_down):
    count = tokens.shape[0]
    hidden, cols = w_gate.shape[1:]
    tiles = hidden // 128
    rows = count // WAVES
    half = 8 * rows
    bf16, f32 = jnp.bfloat16, jnp.float32
    dma = pltpu.SemaphoreType.DMA
    vmem = pl.BlockSpec(memory_space=pltpu.VMEM)
    anywhere = pl.BlockSpec(memory_space=pl.ANY)
    flops = 2 * 16 * count * hidden * cols * 3
    return pl.pallas_call(
        kernel,
        out_shape=jax.ShapeDtypeStruct((count, cols), bf16),
        in_specs=[anywhere, vmem, vmem, anywhere, anywhere, anywhere],
        out_specs=vmem,
        scratch_shapes=[
            pltpu.VMEM((WAVES, 16, rows, cols), bf16),
            pltpu.VMEM((tiles, 2, 128, cols), bf16),
            pltpu.VMEM((hidden, cols), bf16),
            pltpu.VMEM((4, 4, 8, 128), f32),
            pltpu.VMEM((WAVES, 16, rows // 8, 8, 128), f32),
            pltpu.VMEM((WAVES, tiles, half, 256), bf16),
            pltpu.VMEM((WAVES, tiles, half, 256), bf16),
            pltpu.VMEM((WAVES, 2, half, hidden), bf16),
            pltpu.VMEM((WAVES, 16, rows, cols), bf16),
            pltpu.VMEM((WAVES, 3, 4, rows, cols), bf16),
            pltpu.VMEM((WAVES, 4, rows, cols), bf16),
            pltpu.VMEM((WAVES, 4, rows, cols), bf16),
            dma((3,)), dma((WAVES,)),
            dma((WAVES, 4, 4)), dma((WAVES, 4, 4)),
            dma((7,)), dma((7,)),
            dma((WAVES, tiles)), dma((WAVES, tiles)),
            dma((WAVES, tiles)), dma((WAVES, tiles)),
            dma((WAVES, 3, 4)), dma((WAVES, 3, 4)),
            dma((WAVES, 4)), dma((WAVES, 4)),
        ],
        compiler_params=pltpu.CompilerParams(
            collective_id=0, has_side_effects=True, vmem_limit_bytes=52 * 1024 * 1024
        ),
        cost_estimate=pl.CostEstimate(
            flops=flops, bytes_accessed=3 * hidden * cols * 2, transcendentals=8 * count * hidden
        ),
    )(
        tokens, routes, route_weight,
        w_gate.reshape(tiles, 128, cols), w_up.reshape(tiles, 128, cols), w_down[0],
    )


def solution(mesh):
    chips = mesh.shape["wide"] == 16 and mesh.shape["narrow"] == 2
    return jax.shard_map(
        gather_plan if chips else slots_plan,
        mesh=mesh,
        in_specs=(
            P("wide", None),
            P("wide", None),
            P("wide", None),
            P("wide", None, "narrow"),
            P("wide", None, "narrow"),
            P("wide", None, "narrow"),
        ),
        out_specs=P("wide", "narrow"),
        check_vma=False,
    )
```

```python
import jax
import jax.numpy as jnp
from jax import lax
from jax.experimental import pallas as pl
from jax.experimental.pallas import tpu as pltpu
from jax.sharding import PartitionSpec as P


def slot_numbers(routes, experts):
    flat_routes = routes.reshape(-1)
    onehot = (flat_routes[:, None] == jnp.arange(experts, dtype=jnp.int32)[None, :]).astype(
        jnp.int32
    )
    before = jnp.cumsum(onehot, 0) - onehot
    return jnp.sum(before * onehot, 1).reshape(routes.shape)


def slots_plan(tokens, routes, route_weight, w_gate, w_up, w_down):
    tok_count = tokens.shape[0]
    model_width = tokens.shape[1]
    wide_count = lax.axis_size("wide")
    narrow_count = lax.axis_size("narrow")
    local_experts = w_gate.shape[0]
    experts = local_experts * wide_count
    capacity = max(2, (11 * tok_count + experts - 1) // experts)
    column_width = model_width // narrow_count
    slot_index = slot_numbers(routes, experts)
    target = routes * capacity + slot_index
    lane_ids = jnp.arange(experts * capacity, dtype=jnp.int32)
    picker = jnp.sum((lane_ids[:, None, None] == target[None, :, :]).astype(jnp.int32), 2).astype(
        jnp.bfloat16
    )
    columns = lax.dynamic_slice_in_dim(
        tokens, lax.axis_index("narrow") * column_width, column_width, 1
    )
    outgoing = jnp.dot(picker, columns, preferred_element_type=jnp.float32).astype(jnp.bfloat16)
    outgoing = outgoing.reshape(experts, capacity, column_width)
    received = lax.all_to_all(outgoing, "wide", split_axis=0, concat_axis=1, tiled=True)
    expert_rows = received[0]
    slot_total = expert_rows.shape[0]
    gate_matrix = w_gate[0]
    up_matrix = w_up[0]
    down_matrix = w_down[0]
    gate_term = jnp.einsum(
        "sc,fc->fs", expert_rows, gate_matrix, preferred_element_type=jnp.float32
    )
    up_term = jnp.einsum("sc,fc->fs", expert_rows, up_matrix, preferred_element_type=jnp.float32)
    sums = lax.psum_scatter(
        jnp.concatenate([gate_term, up_term], 1).astype(jnp.bfloat16),
        "narrow",
        scatter_dimension=0,
        tiled=True,
    ).astype(jnp.float32)
    hidden = (jax.nn.silu(sums[:, :slot_total]) * sums[:, slot_total:]).astype(jnp.bfloat16)
    produced = jnp.einsum(
        "fs,fc->sc",
        lax.all_gather(hidden, "narrow", axis=0, tiled=True),
        down_matrix,
        preferred_element_type=jnp.float32,
    )
    expert_out = produced.astype(jnp.bfloat16).reshape(local_experts, slot_total, column_width)
    returned = lax.all_to_all(expert_out, "wide", split_axis=1, concat_axis=0, tiled=True)
    flat_rows = returned.reshape(experts * capacity, column_width)
    picked = jnp.take(flat_rows, target, axis=0).astype(jnp.float32)
    combined = jnp.sum(picked * route_weight[:, :, None], 1)
    return combined.astype(jnp.bfloat16)


WAVES = 2
LAG = 3
NT = (((1,), (1,)), ((), ()))
NN = (((1,), (0,)), ((), ()))


def place(column, z):
    return (z // 2) * 8 + column * 2 + z % 2


def kernel(
    tokens, routes, weights, gate_hbm, up_hbm, down_hbm, out,
    tok, gate_up, down, coef, scale, gsend, grecv, hid, part, back, zsend, zrecv,
    load_sem, own_sem, ag_send, ag_recv, cf_send, cf_recv,
    g_send, g_recv, h_send, h_recv, rs_send, rs_recv, z_send, z_recv,
):
    w = lax.axis_index("wide")
    n = lax.axis_index("narrow")
    z = w // 4
    x_peer = w + 1 - 2 * (w % 2)
    y_peer = w + 2 - 4 * ((w // 2) % 2)
    tiles = gate_up.shape[0]
    rows = tok.shape[2]
    half_rows = 8 * rows
    cols = tok.shape[3]

    def copy(src, dst, send, recv, wide, narrow=n):
        return pltpu.make_async_remote_copy(
            src_ref=src, dst_ref=dst, send_sem=send, recv_sem=recv,
            device_id=(wide, narrow), device_id_type=pl.DeviceIdType.MESH,
        )

    def arrived(dst, recv, wide=x_peer):
        copy(dst, dst, recv, recv, wide).wait_recv()

    sent = []

    def send(src, dst, send_sem, recv_sem, wide, narrow=n):
        c = copy(src, dst, send_sem, recv_sem, wide, narrow)
        c.start()
        sent.append(c)

    def z_peer(k):
        return (w + 4 * k) % 16

    barrier = pltpu.get_barrier_semaphore()
    for wide, narrow in [(z_peer(k), n) for k in (1, 2, 3)] + [(x_peer, n), (y_peer, n), (w, 1 - n)]:
        pl.semaphore_signal(barrier, inc=1, device_id=(wide, narrow), device_id_type=pl.DeviceIdType.MESH)
    loads = [
        pltpu.make_async_copy(gate_hbm, gate_up.at[:, 0], load_sem.at[0]),
        pltpu.make_async_copy(up_hbm, gate_up.at[:, 1], load_sem.at[1]),
        pltpu.make_async_copy(down_hbm, down, load_sem.at[2]),
    ]
    own_block = [tokens.at[pl.ds(v * rows, rows), pl.ds(pl.multiple_of(n * cols, cols), cols)] for v in range(WAVES)]
    own_copy = [
        pltpu.make_async_copy(own_block[v], tok.at[v, place(0, z)], own_sem.at[v]) for v in range(WAVES)
    ]
    pl.semaphore_wait(barrier, 6)

    def send_z(v):
        for k in (1, 3, 2):
            send(own_block[v], tok.at[v, place(0, z)], ag_send.at[v, 0, k], ag_recv.at[v, 0, z], z_peer(k))

    def send_xy(v, src, from_z):
        send(src, tok.at[v, place(1, from_z)], ag_send.at[v, 1, from_z], ag_recv.at[v, 1, from_z], x_peer)
        send(src, tok.at[v, place(2, from_z)], ag_send.at[v, 2, from_z], ag_recv.at[v, 2, from_z], y_peer)

    def pass_column(v):
        for k in (1, 3, 2):
            from_z = (z + k) % 4
            block = tok.at[v, place(0, from_z)]
            arrived(block, ag_recv.at[v, 0, from_z])
            send_xy(v, block, from_z)

    def pass_diagonal(v):
        for low in (0, 1):
            for h in (0, 1):
                from_z = 2 * h + low
                block = tok.at[v, place(1 + h, from_z)]
                arrived(block, ag_recv.at[v, 1 + h, from_z])
                send(
                    block, tok.at[v, place(3, from_z)], ag_send.at[v, 3, from_z], ag_recv.at[v, 3, from_z],
                    y_peer if h == 0 else x_peer,
                )

    def gather_rest(v):
        for low in (0, 1):
            for h in (0, 1):
                from_z = 2 * h + low
                arrived(tok.at[v, place(2 - h, from_z)], ag_recv.at[v, 2 - h, from_z])
                arrived(tok.at[v, place(3, from_z)], ag_recv.at[v, 3, from_z])
        own_copy[v].wait()

    send_z(0)
    send_xy(0, own_block[0], z)
    send_z(1)
    for c in own_copy + loads:
        c.start()

    count = routes.shape[1]
    diagonal = lax.broadcasted_iota(jnp.int32, (count, count), 0) == lax.broadcasted_iota(
        jnp.int32, (count, count), 1
    )

    def as_column(row):
        return jnp.sum(jnp.where(diagonal, jnp.broadcast_to(row, (count, count)), 0.0), 1, keepdims=True)

    lane = lax.broadcasted_iota(jnp.int32, (8, 128), 1).astype(jnp.float32)
    packed = jnp.zeros((8, 128), jnp.float32)
    for k in range(routes.shape[0]):
        chosen = as_column(routes[k : k + 1, :].astype(jnp.float32))
        amount = as_column(weights[k : k + 1, :])
        for g in range(count // 8):
            packed += jnp.where(lane == chosen[8 * g : 8 * g + 8] + 16.0 * g, amount[8 * g : 8 * g + 8], 0.0)
    coef[0, z] = packed
    for k in (1, 2, 3):
        send(coef.at[0, z], coef.at[0, z], cf_send.at[k], cf_recv.at[z], z_peer(k))

    pass_column(0)
    send_xy(1, own_block[1], z)
    pass_diagonal(0)
    pass_column(1)
    for k in (1, 2, 3):
        from_z = (z + k) % 4
        arrived(coef.at[0, from_z], cf_recv.at[from_z])
    send(coef.at[0], coef.at[1], cf_send.at[4], cf_recv.at[4], x_peer)
    send(coef.at[0], coef.at[2], cf_send.at[5], cf_recv.at[5], y_peer)
    for c in loads[:2]:
        c.wait()
    gather_rest(0)

    def tile(i):
        return gate_up[i].reshape(2 * gate_up.shape[2], cols)

    def add_tile(v, i):
        x = tok[v].reshape(2 * half_rows, cols)
        sums = lax.dot_general(x, tile(i), NT, preferred_element_type=jnp.float32)
        gsend[v, i] = sums.astype(jnp.bfloat16).reshape(2, half_rows, 256)
        copy(gsend.at[v, i, 1 - n], grecv.at[v, i], g_send.at[v, i], g_recv.at[v, i], w, 1 - n).start()

    def hide_tile(v, i):
        arrived(grecv.at[v, i], g_recv.at[v, i])
        sums = gsend[v, i, n].astype(jnp.float32) + grecv[v, i].astype(jnp.float32)
        gate, up = sums[:, :128], sums[:, 128:]
        lanes = pl.ds(pl.multiple_of(i * 128, 128), 128)
        hid[v, n, :, lanes] = (gate / (1.0 + jnp.exp(-gate)) * up).astype(jnp.bfloat16)
        there = hid.at[v, n, :, lanes]
        copy(there, there, h_send.at[v, i], h_recv.at[v, i], w, 1 - n).start()

    def hidden_units(v):
        @pl.loop(0, LAG)
        def _(i):
            add_tile(v, i)

        @pl.loop(LAG, tiles)
        def _(i):
            add_tile(v, i)
            hide_tile(v, i - LAG)

        @pl.loop(tiles - LAG, tiles)
        def _(i):
            hide_tile(v, i)

    def outputs(v, h):
        column = scale[v, pl.ds(8 * h, 8)].reshape(half_rows, 128)[:, 0:1]

        @pl.loop(0, cols // 256)
        def _(i):
            lanes = pl.ds(pl.multiple_of(i * 256, 256), 256)
            acc = lax.dot_general(hid[v, h], down[:, lanes], NN, preferred_element_type=jnp.float32)
            part[v, pl.ds(8 * h, 8), :, lanes] = (acc * column).astype(jnp.bfloat16).reshape(8, rows, 256)

    def other_hidden(v):
        @pl.loop(0, tiles)
        def _(i):
            lanes = pl.ds(pl.multiple_of(i * 128, 128), 128)
            arrived(hid.at[v, 1 - n, :, lanes], h_recv.at[v, i])

    def send_half(v, h):
        peer = x_peer + h * (y_peer - x_peer)
        for low in (0, 1):
            at = 2 * h + low
            send(part.at[v, place(3, at)], back.at[v, 0, at], rs_send.at[v, 0, at], rs_recv.at[v, 0, at], peer)
        for low in (0, 1):
            at = 2 * h + low
            send(
                part.at[v, place(1 + h, at)], back.at[v, 1 + h, at],
                rs_send.at[v, 1 + h, at], rs_recv.at[v, 1 + h, at], peer,
            )

    def relay_sums(v):
        for low in (0, 1):
            for h in (0, 1):
                at = 2 * h + low
                arrived(back.at[v, 0, at], rs_recv.at[v, 0, at])
                mine = part[v, place(2 - h, at)].astype(jnp.float32)
                part[v, place(2 - h, at)] = (mine + back[v, 0, at].astype(jnp.float32)).astype(jnp.bfloat16)
                send(
                    part.at[v, place(2 - h, at)], back.at[v, 2 - h, at],
                    rs_send.at[v, 2 - h, at], rs_recv.at[v, 2 - h, at], y_peer if h == 0 else x_peer,
                )

    def column_sums(v):
        for k in (2, 1, 3, 0):
            at = (z + k) % 4
            arrived(back.at[v, 1, at], rs_recv.at[v, 1, at])
            arrived(back.at[v, 2, at], rs_recv.at[v, 2, at])
            total = part[v, place(0, at)].astype(jnp.float32)
            total += back[v, 1, at].astype(jnp.float32) + back[v, 2, at].astype(jnp.float32)
            if k == 0:
                zrecv[v, z] = total.astype(jnp.bfloat16)
            else:
                zsend[v, k] = total.astype(jnp.bfloat16)
                send(zsend.at[v, k], zrecv.at[v, z], z_send.at[v, k], z_recv.at[v, z], z_peer(k))

    def finish(v):
        for k in (1, 3, 2):
            at = (z + k) % 4
            arrived(zrecv.at[v, at], z_recv.at[v, at])
        total = zrecv[v, 0].astype(jnp.float32) + zrecv[v, 1].astype(jnp.float32)
        total += zrecv[v, 2].astype(jnp.float32) + zrecv[v, 3].astype(jnp.float32)
        out[pl.ds(v * rows, rows), :] = total.astype(jnp.bfloat16)

    hidden_units(0)
    arrived(coef.at[1], cf_recv.at[4])
    send(coef.at[1], coef.at[3], cf_send.at[6], cf_recv.at[6], y_peer)
    pass_diagonal(1)
    arrived(coef.at[2], cf_recv.at[5])
    arrived(coef.at[3], cf_recv.at[6])
    lane = lax.broadcasted_iota(jnp.int32, (4, 8, 128), 2)
    for column in range(4):
        block = coef[column]
        for g in range(tokens.shape[0] // 8):
            mine = jnp.sum(jnp.where(lane == 16 * g + w, block, 0.0), 2, keepdims=True)
            mine = jnp.broadcast_to(mine, (4, 8, 128))
            for at in range(4):
                scale[g * 8 // rows, place(column, at), g % (rows // 8)] = mine[at]
    loads[2].wait()
    outputs(0, n)
    send_half(0, n)
    other_hidden(0)
    outputs(0, 1 - n)
    send_half(0, 1 - n)

    gather_rest(1)
    hidden_units(1)
    relay_sums(0)
    column_sums(0)
    outputs(1, n)
    send_half(1, n)
    other_hidden(1)
    outputs(1, 1 - n)
    send_half(1, 1 - n)
    relay_sums(1)
    column_sums(1)
    finish(0)
    finish(1)

    for c in sent:
        c.wait_send()
    for v in range(WAVES):

        @pl.loop(0, tiles)
        def _(i):
            lanes = pl.ds(pl.multiple_of(i * 128, 128), 128)
            there = hid.at[v, n, :, lanes]
            copy(gsend.at[v, i, 1 - n], grecv.at[v, i], g_send.at[v, i], g_recv.at[v, i], w, 1 - n).wait_send()
            copy(there, there, h_send.at[v, i], h_recv.at[v, i], w, 1 - n).wait_send()


def gather_plan(tokens, routes, route_weight, w_gate, w_up, w_down):
    count = tokens.shape[0]
    hidden, cols = w_gate.shape[1:]
    tiles = hidden // 128
    rows = count // WAVES
    half = 8 * rows
    bf16, f32 = jnp.bfloat16, jnp.float32
    dma = pltpu.SemaphoreType.DMA
    vmem = pl.BlockSpec(memory_space=pltpu.VMEM)
    anywhere = pl.BlockSpec(memory_space=pltpu.HBM)
    flops = 2 * 16 * count * hidden * cols * 3
    return pl.pallas_call(
        kernel,
        out_shape=jax.ShapeDtypeStruct((count, cols), bf16),
        in_specs=[anywhere, vmem, vmem, anywhere, anywhere, anywhere],
        out_specs=vmem,
        scratch_shapes=[
            pltpu.VMEM((WAVES, 16, rows, cols), bf16),
            pltpu.VMEM((tiles, 2, 128, cols), bf16),
            pltpu.VMEM((hidden, cols), bf16),
            pltpu.VMEM((4, 4, 8, 128), f32),
            pltpu.VMEM((WAVES, 16, rows // 8, 8, 128), f32),
            pltpu.VMEM((WAVES, tiles, 2, half, 256), bf16),
            pltpu.VMEM((WAVES, tiles, half, 256), bf16),
            pltpu.VMEM((WAVES, 2, half, hidden), bf16),
            pltpu.VMEM((WAVES, 16, rows, cols), bf16),
            pltpu.VMEM((WAVES, 3, 4, rows, cols), bf16),
            pltpu.VMEM((WAVES, 4, rows, cols), bf16),
            pltpu.VMEM((WAVES, 4, rows, cols), bf16),
            dma((3,)), dma((WAVES,)),
            dma((WAVES, 4, 4)), dma((WAVES, 4, 4)),
            dma((7,)), dma((7,)),
            dma((WAVES, tiles)), dma((WAVES, tiles)),
            dma((WAVES, tiles)), dma((WAVES, tiles)),
            dma((WAVES, 3, 4)), dma((WAVES, 3, 4)),
            dma((WAVES, 4)), dma((WAVES, 4)),
        ],
        compiler_params=pltpu.CompilerParams(
            collective_id=0, has_side_effects=True, vmem_limit_bytes=52 * 1024 * 1024
        ),
        cost_estimate=pl.CostEstimate(
            flops=flops, bytes_accessed=3 * hidden * cols * 2, transcendentals=8 * count * hidden
        ),
    )(
        tokens, routes.T, route_weight.T,
        w_gate.reshape(tiles, 128, cols), w_up.reshape(tiles, 128, cols), w_down[0],
    )


def solution(mesh):
    chips = mesh.shape["wide"] == 16 and mesh.shape["narrow"] == 2
    return jax.shard_map(
        gather_plan if chips else slots_plan,
        mesh=mesh,
        in_specs=(
            P("wide", None),
            P("wide", None),
            P("wide", None),
            P("wide", None, "narrow"),
            P("wide", None, "narrow"),
            P("wide", None, "narrow"),
        ),
        out_specs=P("wide", "narrow"),
        check_vma=False,
    )
```

```python
import jax
import jax.numpy as jnp
from jax import lax
from jax.experimental import pallas as pl
from jax.experimental.pallas import tpu as pltpu
from jax.sharding import PartitionSpec as P


def slot_numbers(routes, experts):
    flat_routes = routes.reshape(-1)
    onehot = (flat_routes[:, None] == jnp.arange(experts, dtype=jnp.int32)[None, :]).astype(
        jnp.int32
    )
    before = jnp.cumsum(onehot, 0) - onehot
    return jnp.sum(before * onehot, 1).reshape(routes.shape)


def slots_plan(tokens, routes, route_weight, w_gate, w_up, w_down):
    tok_count = tokens.shape[0]
    model_width = tokens.shape[1]
    wide_count = lax.axis_size("wide")
    narrow_count = lax.axis_size("narrow")
    local_experts = w_gate.shape[0]
    experts = local_experts * wide_count
    capacity = max(2, (11 * tok_count + experts - 1) // experts)
    column_width = model_width // narrow_count
    slot_index = slot_numbers(routes, experts)
    target = routes * capacity + slot_index
    lane_ids = jnp.arange(experts * capacity, dtype=jnp.int32)
    picker = jnp.sum((lane_ids[:, None, None] == target[None, :, :]).astype(jnp.int32), 2).astype(
        jnp.bfloat16
    )
    columns = lax.dynamic_slice_in_dim(
        tokens, lax.axis_index("narrow") * column_width, column_width, 1
    )
    outgoing = jnp.dot(picker, columns, preferred_element_type=jnp.float32).astype(jnp.bfloat16)
    outgoing = outgoing.reshape(experts, capacity, column_width)
    received = lax.all_to_all(outgoing, "wide", split_axis=0, concat_axis=1, tiled=True)
    expert_rows = received[0]
    slot_total = expert_rows.shape[0]
    gate_matrix = w_gate[0]
    up_matrix = w_up[0]
    down_matrix = w_down[0]
    gate_term = jnp.einsum(
        "sc,fc->fs", expert_rows, gate_matrix, preferred_element_type=jnp.float32
    )
    up_term = jnp.einsum("sc,fc->fs", expert_rows, up_matrix, preferred_element_type=jnp.float32)
    sums = lax.psum_scatter(
        jnp.concatenate([gate_term, up_term], 1).astype(jnp.bfloat16),
        "narrow",
        scatter_dimension=0,
        tiled=True,
    ).astype(jnp.float32)
    hidden = (jax.nn.silu(sums[:, :slot_total]) * sums[:, slot_total:]).astype(jnp.bfloat16)
    produced = jnp.einsum(
        "fs,fc->sc",
        lax.all_gather(hidden, "narrow", axis=0, tiled=True),
        down_matrix,
        preferred_element_type=jnp.float32,
    )
    expert_out = produced.astype(jnp.bfloat16).reshape(local_experts, slot_total, column_width)
    returned = lax.all_to_all(expert_out, "wide", split_axis=1, concat_axis=0, tiled=True)
    flat_rows = returned.reshape(experts * capacity, column_width)
    picked = jnp.take(flat_rows, target, axis=0).astype(jnp.float32)
    combined = jnp.sum(picked * route_weight[:, :, None], 1)
    return combined.astype(jnp.bfloat16)


WAVES = 4
LAG = 3
NT = (((1,), (1,)), ((), ()))
NN = (((1,), (0,)), ((), ()))


def place(column, z):
    return (z // 2) * 8 + column * 2 + z % 2


def kernel(
    tokens, routes_hbm, weights_hbm, gate_hbm, up_hbm, down_hbm, out,
    routes, weights, tok, gate_up, down, coef, scale, gsend, grecv, hid, part, back, zsend, zrecv,
    load_sem, own_sem, ag_send, ag_recv, cf_send, cf_recv,
    g_send, g_recv, h_send, h_recv, rs_send, rs_recv, z_send, z_recv,
):
    w = lax.axis_index("wide")
    n = lax.axis_index("narrow")
    z = w // 4
    x_peer = w + 1 - 2 * (w % 2)
    y_peer = w + 2 - 4 * ((w // 2) % 2)
    tiles = gate_up.shape[0]
    rows = tok.shape[2]
    half_rows = 8 * rows
    cols = tok.shape[3]

    def copy(src, dst, send, recv, wide, narrow=n):
        return pltpu.make_async_remote_copy(
            src_ref=src, dst_ref=dst, send_sem=send, recv_sem=recv,
            device_id=(wide, narrow), device_id_type=pl.DeviceIdType.MESH,
        )

    def arrived(dst, recv, wide=x_peer):
        copy(dst, dst, recv, recv, wide).wait_recv()

    sent = []

    def send(src, dst, send_sem, recv_sem, wide, narrow=n):
        c = copy(src, dst, send_sem, recv_sem, wide, narrow)
        c.start()
        sent.append(c)

    def z_peer(k):
        return (w + 4 * k) % 16

    barrier = pltpu.get_barrier_semaphore()
    for wide, narrow in [(z_peer(k), n) for k in (1, 2, 3)] + [(x_peer, n), (y_peer, n), (w, 1 - n)]:
        pl.semaphore_signal(barrier, inc=1, device_id=(wide, narrow), device_id_type=pl.DeviceIdType.MESH)
    loads = [
        pltpu.make_async_copy(gate_hbm, gate_up.at[:, 0], load_sem.at[0]),
        pltpu.make_async_copy(up_hbm, gate_up.at[:, 1], load_sem.at[1]),
        pltpu.make_async_copy(down_hbm, down, load_sem.at[2]),
        pltpu.make_async_copy(routes_hbm, routes, load_sem.at[3]),
        pltpu.make_async_copy(weights_hbm, weights, load_sem.at[4]),
    ]
    own_block = [tokens.at[pl.ds(v * rows, rows), pl.ds(pl.multiple_of(n * cols, cols), cols)] for v in range(WAVES)]
    own_copy = [
        pltpu.make_async_copy(own_block[v], tok.at[v, place(0, z)], own_sem.at[v]) for v in range(WAVES)
    ]
    for c in loads[3:]:
        c.start()
    pl.semaphore_wait(barrier, 6)

    def send_z(v):
        for k in (1, 3, 2):
            send(own_block[v], tok.at[v, place(0, z)], ag_send.at[v, 0, k], ag_recv.at[v, 0, z], z_peer(k))

    def send_xy(v, src, from_z):
        send(src, tok.at[v, place(1, from_z)], ag_send.at[v, 1, from_z], ag_recv.at[v, 1, from_z], x_peer)
        send(src, tok.at[v, place(2, from_z)], ag_send.at[v, 2, from_z], ag_recv.at[v, 2, from_z], y_peer)

    def pass_column(v):
        for k in (1, 3, 2):
            from_z = (z + k) % 4
            block = tok.at[v, place(0, from_z)]
            arrived(block, ag_recv.at[v, 0, from_z])
            send_xy(v, block, from_z)

    def pass_diagonal(v):
        for k in (0, 1, 3, 2):
            from_z = (z + k) % 4
            h = from_z // 2
            block = tok.at[v, place(1 + h, from_z)]
            arrived(block, ag_recv.at[v, 1 + h, from_z])
            send(
                block, tok.at[v, place(3, from_z)], ag_send.at[v, 3, from_z], ag_recv.at[v, 3, from_z],
                y_peer + h * (x_peer - y_peer),
            )

    def gather_rest(v):
        for low in (0, 1):
            for h in (0, 1):
                from_z = 2 * h + low
                arrived(tok.at[v, place(2 - h, from_z)], ag_recv.at[v, 2 - h, from_z])
                arrived(tok.at[v, place(3, from_z)], ag_recv.at[v, 3, from_z])
        own_copy[v].wait()

    def send_own(v):
        send_z(v)
        send_xy(v, own_block[v], z)

    send_own(0)
    for c in own_copy + loads[:3]:
        c.start()
    for c in loads[3:]:
        c.wait()

    count = routes.shape[1]
    diagonal = lax.broadcasted_iota(jnp.int32, (count, count), 0) == lax.broadcasted_iota(
        jnp.int32, (count, count), 1
    )

    def as_column(row):
        return jnp.sum(jnp.where(diagonal, jnp.broadcast_to(row, (count, count)), 0.0), 1, keepdims=True)

    lane = lax.broadcasted_iota(jnp.int32, (8, 128), 1).astype(jnp.float32)
    packed = jnp.zeros((8, 128), jnp.float32)
    for k in range(routes.shape[0]):
        chosen = as_column(routes[k : k + 1, :].astype(jnp.float32))
        amount = as_column(weights[k : k + 1, :])
        for g in range(count // 8):
            packed += jnp.where(lane == chosen[8 * g : 8 * g + 8] + 16.0 * g, amount[8 * g : 8 * g + 8], 0.0)
    coef[0, z] = packed
    for k in (1, 2, 3):
        send(coef.at[0, z], coef.at[0, z], cf_send.at[k], cf_recv.at[z], z_peer(k))

    pass_column(0)
    send_own(1)
    pass_diagonal(0)
    pass_column(1)
    send_own(2)
    for k in (1, 2, 3):
        from_z = (z + k) % 4
        arrived(coef.at[0, from_z], cf_recv.at[from_z])
    send(coef.at[0], coef.at[1], cf_send.at[4], cf_recv.at[4], x_peer)
    send(coef.at[0], coef.at[2], cf_send.at[5], cf_recv.at[5], y_peer)
    for c in loads[:2]:
        c.wait()

    def tile(i):
        return gate_up[i].reshape(2 * gate_up.shape[2], cols)

    def add_tile(v, i):
        x = tok[v].reshape(2 * half_rows, cols)
        sums = lax.dot_general(x, tile(i), NT, preferred_element_type=jnp.float32)
        gsend[v, i] = sums.astype(jnp.bfloat16).reshape(2, half_rows, 256)
        copy(gsend.at[v, i, 1 - n], grecv.at[v, i], g_send.at[v, i], g_recv.at[v, i], w, 1 - n).start()

    def hide_tile(v, i):
        arrived(grecv.at[v, i], g_recv.at[v, i])
        sums = gsend[v, i, n].astype(jnp.float32) + grecv[v, i].astype(jnp.float32)
        gate, up = sums[:, :128], sums[:, 128:]
        lanes = pl.ds(pl.multiple_of(i * 128, 128), 128)
        hid[v, n, :, lanes] = (gate / (1.0 + jnp.exp(-gate)) * up).astype(jnp.bfloat16)
        there = hid.at[v, n, :, lanes]
        copy(there, there, h_send.at[v, i], h_recv.at[v, i], w, 1 - n).start()

    def hidden_units(v):
        @pl.loop(0, LAG)
        def _(i):
            add_tile(v, i)

        @pl.loop(LAG, tiles)
        def _(i):
            add_tile(v, i)
            hide_tile(v, i - LAG)

        @pl.loop(tiles - LAG, tiles)
        def _(i):
            hide_tile(v, i)

    def outputs(v, h):
        column = scale[v, pl.ds(8 * h, 8)].reshape(half_rows, 128)[:, 0:1]

        @pl.loop(0, cols // 256)
        def _(i):
            lanes = pl.ds(pl.multiple_of(i * 256, 256), 256)
            acc = lax.dot_general(hid[v, h], down[:, lanes], NN, preferred_element_type=jnp.float32)
            part[v, pl.ds(8 * h, 8), :, lanes] = (acc * column).astype(jnp.bfloat16).reshape(8, rows, 256)

    def other_hidden(v):
        @pl.loop(0, tiles)
        def _(i):
            lanes = pl.ds(pl.multiple_of(i * 128, 128), 128)
            arrived(hid.at[v, 1 - n, :, lanes], h_recv.at[v, i])

    def send_half(v, h):
        peer = x_peer + h * (y_peer - x_peer)
        for low in (0, 1):
            at = 2 * h + low
            send(part.at[v, place(3, at)], back.at[v, 0, at], rs_send.at[v, 0, at], rs_recv.at[v, 0, at], peer)
        for low in (0, 1):
            at = 2 * h + low
            send(
                part.at[v, place(1 + h, at)], back.at[v, 1 + h, at],
                rs_send.at[v, 1 + h, at], rs_recv.at[v, 1 + h, at], peer,
            )

    def relay_sums(v):
        for low in (0, 1):
            for h in (0, 1):
                at = 2 * h + low
                arrived(back.at[v, 0, at], rs_recv.at[v, 0, at])
                mine = part[v, place(2 - h, at)].astype(jnp.float32)
                part[v, place(2 - h, at)] = (mine + back[v, 0, at].astype(jnp.float32)).astype(jnp.bfloat16)
                send(
                    part.at[v, place(2 - h, at)], back.at[v, 2 - h, at],
                    rs_send.at[v, 2 - h, at], rs_recv.at[v, 2 - h, at], y_peer if h == 0 else x_peer,
                )

    def column_sums(v):
        for k in (2, 1, 3, 0):
            at = (z + k) % 4
            arrived(back.at[v, 1, at], rs_recv.at[v, 1, at])
            arrived(back.at[v, 2, at], rs_recv.at[v, 2, at])
            total = part[v, place(0, at)].astype(jnp.float32)
            total += back[v, 1, at].astype(jnp.float32) + back[v, 2, at].astype(jnp.float32)
            if k == 0:
                zrecv[v, z] = total.astype(jnp.bfloat16)
            else:
                zsend[v, k] = total.astype(jnp.bfloat16)
                send(zsend.at[v, k], zrecv.at[v, z], z_send.at[v, k], z_recv.at[v, z], z_peer(k))

    def finish(v):
        for k in (1, 3, 2):
            at = (z + k) % 4
            arrived(zrecv.at[v, at], z_recv.at[v, at])
        total = zrecv[v, 0].astype(jnp.float32) + zrecv[v, 1].astype(jnp.float32)
        total += zrecv[v, 2].astype(jnp.float32) + zrecv[v, 3].astype(jnp.float32)
        out[pl.ds(v * rows, rows), :] = total.astype(jnp.bfloat16)

    def make_scale():
        arrived(coef.at[2], cf_recv.at[5])
        arrived(coef.at[3], cf_recv.at[6])
        lane = lax.broadcasted_iota(jnp.int32, (4, 8, 128), 2)
        for column in range(4):
            block = coef[column]
            for g in range(tokens.shape[0] // 8):
                mine = jnp.sum(jnp.where(lane == 16 * g + w, block, 0.0), 2, keepdims=True)
                mine = jnp.broadcast_to(mine, (4, 8, 128))
                for at in range(4):
                    scale[g * 8 // rows, place(column, at), g % (rows // 8)] = mine[at]

    def give(v):
        outputs(v, n)
        send_half(v, n)
        other_hidden(v)
        outputs(v, 1 - n)
        send_half(v, 1 - n)

    gather_rest(0)
    hidden_units(0)
    arrived(coef.at[1], cf_recv.at[4])
    send(coef.at[1], coef.at[3], cf_send.at[6], cf_recv.at[6], y_peer)
    pass_diagonal(1)
    pass_column(2)
    send_own(3)
    make_scale()
    loads[2].wait()
    give(0)

    gather_rest(1)
    hidden_units(1)
    pass_diagonal(2)
    pass_column(3)
    relay_sums(0)
    give(1)

    gather_rest(2)
    hidden_units(2)
    pass_diagonal(3)
    relay_sums(1)
    column_sums(0)
    give(2)

    gather_rest(3)
    hidden_units(3)
    relay_sums(2)
    column_sums(1)
    give(3)

    column_sums(2)
    relay_sums(3)
    column_sums(3)
    for v in range(WAVES):
        finish(v)

    for c in sent:
        c.wait_send()
    for v in range(WAVES):

        @pl.loop(0, tiles)
        def _(i):
            lanes = pl.ds(pl.multiple_of(i * 128, 128), 128)
            there = hid.at[v, n, :, lanes]
            copy(gsend.at[v, i, 1 - n], grecv.at[v, i], g_send.at[v, i], g_recv.at[v, i], w, 1 - n).wait_send()
            copy(there, there, h_send.at[v, i], h_recv.at[v, i], w, 1 - n).wait_send()


def gather_plan(tokens, routes, route_weight, w_gate, w_up, w_down):
    count = tokens.shape[0]
    hidden, cols = w_gate.shape[1:]
    tiles = hidden // 128
    rows = count // WAVES
    half = 8 * rows
    bf16, f32 = jnp.bfloat16, jnp.float32
    dma = pltpu.SemaphoreType.DMA
    vmem = pl.BlockSpec(memory_space=pltpu.VMEM)
    anywhere = pl.BlockSpec(memory_space=pl.ANY)
    flops = 2 * 16 * count * hidden * cols * 3
    return pl.pallas_call(
        kernel,
        out_shape=jax.ShapeDtypeStruct((count, cols), bf16),
        in_specs=[anywhere] * 6,
        out_specs=vmem,
        scratch_shapes=[
            pltpu.VMEM((route_weight.shape[1], count), jnp.int32),
            pltpu.VMEM((route_weight.shape[1], count), f32),
            pltpu.VMEM((WAVES, 16, rows, cols), bf16),
            pltpu.VMEM((tiles, 2, 128, cols), bf16),
            pltpu.VMEM((hidden, cols), bf16),
            pltpu.VMEM((4, 4, 8, 128), f32),
            pltpu.VMEM((WAVES, 16, rows // 8, 8, 128), f32),
            pltpu.VMEM((WAVES, tiles, 2, half, 256), bf16),
            pltpu.VMEM((WAVES, tiles, half, 256), bf16),
            pltpu.VMEM((WAVES, 2, half, hidden), bf16),
            pltpu.VMEM((WAVES, 16, rows, cols), bf16),
            pltpu.VMEM((WAVES, 3, 4, rows, cols), bf16),
            pltpu.VMEM((WAVES, 4, rows, cols), bf16),
            pltpu.VMEM((WAVES, 4, rows, cols), bf16),
            dma((5,)), dma((WAVES,)),
            dma((WAVES, 4, 4)), dma((WAVES, 4, 4)),
            dma((7,)), dma((7,)),
            dma((WAVES, tiles)), dma((WAVES, tiles)),
            dma((WAVES, tiles)), dma((WAVES, tiles)),
            dma((WAVES, 3, 4)), dma((WAVES, 3, 4)),
            dma((WAVES, 4)), dma((WAVES, 4)),
        ],
        compiler_params=pltpu.CompilerParams(
            collective_id=0, has_side_effects=True, vmem_limit_bytes=64 * 1024 * 1024 - 128 * 1024
        ),
        cost_estimate=pl.CostEstimate(
            flops=flops, bytes_accessed=3 * hidden * cols * 2, transcendentals=8 * count * hidden
        ),
    )(
        tokens, routes.T, route_weight.T,
        w_gate.reshape(tiles, 128, cols), w_up.reshape(tiles, 128, cols), w_down[0],
    )


def solution(mesh):
    chips = mesh.shape["wide"] == 16 and mesh.shape["narrow"] == 2
    return jax.shard_map(
        gather_plan if chips else slots_plan,
        mesh=mesh,
        in_specs=(
            P("wide", None),
            P("wide", None),
            P("wide", None),
            P("wide", None, "narrow"),
            P("wide", None, "narrow"),
            P("wide", None, "narrow"),
        ),
        out_specs=P("wide", "narrow"),
        check_vma=False,
    )
```

```python
import jax
import jax.numpy as jnp
from jax import lax
from jax.experimental import pallas as pl
from jax.experimental.pallas import tpu as pltpu
from jax.sharding import PartitionSpec as P


def slot_numbers(routes, experts):
    flat_routes = routes.reshape(-1)
    onehot = (flat_routes[:, None] == jnp.arange(experts, dtype=jnp.int32)[None, :]).astype(
        jnp.int32
    )
    before = jnp.cumsum(onehot, 0) - onehot
    return jnp.sum(before * onehot, 1).reshape(routes.shape)


def slots_plan(tokens, routes, route_weight, w_gate, w_up, w_down):
    tok_count = tokens.shape[0]
    model_width = tokens.shape[1]
    wide_count = lax.axis_size("wide")
    narrow_count = lax.axis_size("narrow")
    local_experts = w_gate.shape[0]
    experts = local_experts * wide_count
    capacity = max(2, (11 * tok_count + experts - 1) // experts)
    column_width = model_width // narrow_count
    slot_index = slot_numbers(routes, experts)
    target = routes * capacity + slot_index
    lane_ids = jnp.arange(experts * capacity, dtype=jnp.int32)
    picker = jnp.sum((lane_ids[:, None, None] == target[None, :, :]).astype(jnp.int32), 2).astype(
        jnp.bfloat16
    )
    columns = lax.dynamic_slice_in_dim(
        tokens, lax.axis_index("narrow") * column_width, column_width, 1
    )
    outgoing = jnp.dot(picker, columns, preferred_element_type=jnp.float32).astype(jnp.bfloat16)
    outgoing = outgoing.reshape(experts, capacity, column_width)
    received = lax.all_to_all(outgoing, "wide", split_axis=0, concat_axis=1, tiled=True)
    expert_rows = received[0]
    slot_total = expert_rows.shape[0]
    gate_matrix = w_gate[0]
    up_matrix = w_up[0]
    down_matrix = w_down[0]
    gate_term = jnp.einsum(
        "sc,fc->fs", expert_rows, gate_matrix, preferred_element_type=jnp.float32
    )
    up_term = jnp.einsum("sc,fc->fs", expert_rows, up_matrix, preferred_element_type=jnp.float32)
    sums = lax.psum_scatter(
        jnp.concatenate([gate_term, up_term], 1).astype(jnp.bfloat16),
        "narrow",
        scatter_dimension=0,
        tiled=True,
    ).astype(jnp.float32)
    hidden = (jax.nn.silu(sums[:, :slot_total]) * sums[:, slot_total:]).astype(jnp.bfloat16)
    produced = jnp.einsum(
        "fs,fc->sc",
        lax.all_gather(hidden, "narrow", axis=0, tiled=True),
        down_matrix,
        preferred_element_type=jnp.float32,
    )
    expert_out = produced.astype(jnp.bfloat16).reshape(local_experts, slot_total, column_width)
    returned = lax.all_to_all(expert_out, "wide", split_axis=1, concat_axis=0, tiled=True)
    flat_rows = returned.reshape(experts * capacity, column_width)
    picked = jnp.take(flat_rows, target, axis=0).astype(jnp.float32)
    combined = jnp.sum(picked * route_weight[:, :, None], 1)
    return combined.astype(jnp.bfloat16)


WAVES = 4
LAG = 3
NN = (((1,), (0,)), ((), ()))


def place(column, z):
    return (z // 2) * 8 + column * 2 + z % 2


def kernel(
    tokens, routes_hbm, weights_hbm, gate_hbm, up_hbm, down_hbm, out,
    routes, weights, tok, gate_up, gate_up_t, down, coef, scale, gsend, grecv, hid, part, back, zsend, zrecv,
    load_sem, own_sem, ag_send, ag_recv, cf_send, cf_recv,
    g_send, g_recv, h_send, h_recv, rs_send, rs_recv, z_send, z_recv,
):
    w = lax.axis_index("wide")
    n = lax.axis_index("narrow")
    z = w // 4
    x_peer = w + 1 - 2 * (w % 2)
    y_peer = w + 2 - 4 * ((w // 2) % 2)
    tiles = gate_up.shape[0]
    rows = tok.shape[2]
    half_rows = 8 * rows
    cols = tok.shape[3]

    def copy(src, dst, send, recv, wide, narrow=n):
        return pltpu.make_async_remote_copy(
            src_ref=src, dst_ref=dst, send_sem=send, recv_sem=recv,
            device_id=(wide, narrow), device_id_type=pl.DeviceIdType.MESH,
        )

    def arrived(dst, recv, wide=x_peer):
        copy(dst, dst, recv, recv, wide).wait_recv()

    sent = []

    def send(src, dst, send_sem, recv_sem, wide, narrow=n):
        c = copy(src, dst, send_sem, recv_sem, wide, narrow)
        c.start()
        sent.append(c)

    def z_peer(k):
        return (w + 4 * k) % 16

    barrier = pltpu.get_barrier_semaphore()
    for wide, narrow in [(z_peer(k), n) for k in (1, 2, 3)] + [(x_peer, n), (y_peer, n), (w, 1 - n)]:
        pl.semaphore_signal(barrier, inc=1, device_id=(wide, narrow), device_id_type=pl.DeviceIdType.MESH)
    loads = [
        pltpu.make_async_copy(gate_hbm, gate_up.at[:, 0], load_sem.at[0]),
        pltpu.make_async_copy(up_hbm, gate_up.at[:, 1], load_sem.at[1]),
        pltpu.make_async_copy(down_hbm, down, load_sem.at[2]),
        pltpu.make_async_copy(routes_hbm, routes, load_sem.at[3]),
        pltpu.make_async_copy(weights_hbm, weights, load_sem.at[4]),
    ]
    own_block = [tokens.at[pl.ds(v * rows, rows), pl.ds(pl.multiple_of(n * cols, cols), cols)] for v in range(WAVES)]
    own_copy = [
        pltpu.make_async_copy(own_block[v], tok.at[v, place(0, z)], own_sem.at[v]) for v in range(WAVES)
    ]
    for c in loads[3:]:
        c.start()
    pl.semaphore_wait(barrier, 6)

    def send_z(v):
        for k in (1, 3, 2):
            send(own_block[v], tok.at[v, place(0, z)], ag_send.at[v, 0, k], ag_recv.at[v, 0, z], z_peer(k))

    def send_xy(v, src, from_z):
        send(src, tok.at[v, place(1, from_z)], ag_send.at[v, 1, from_z], ag_recv.at[v, 1, from_z], x_peer)
        send(src, tok.at[v, place(2, from_z)], ag_send.at[v, 2, from_z], ag_recv.at[v, 2, from_z], y_peer)

    def pass_column(v):
        for k in (1, 3, 2):
            from_z = (z + k) % 4
            block = tok.at[v, place(0, from_z)]
            arrived(block, ag_recv.at[v, 0, from_z])
            send_xy(v, block, from_z)

    def pass_diagonal(v):
        for k in (0, 1, 3, 2):
            from_z = (z + k) % 4
            h = from_z // 2
            block = tok.at[v, place(1 + h, from_z)]
            arrived(block, ag_recv.at[v, 1 + h, from_z])
            send(
                block, tok.at[v, place(3, from_z)], ag_send.at[v, 3, from_z], ag_recv.at[v, 3, from_z],
                y_peer + h * (x_peer - y_peer),
            )

    def gather_rest(v):
        for low in (0, 1):
            for h in (0, 1):
                from_z = 2 * h + low
                arrived(tok.at[v, place(2 - h, from_z)], ag_recv.at[v, 2 - h, from_z])
                arrived(tok.at[v, place(3, from_z)], ag_recv.at[v, 3, from_z])
        own_copy[v].wait()

    send_z(0)
    for v in range(WAVES):
        send_xy(v, own_block[v], z)
    for c in own_copy + loads[:3]:
        c.start()
    for c in loads[3:]:
        c.wait()

    def turn_tiles(first, last):
        @pl.loop(first, last)
        def _(i):
            gate_up_t[i] = gate_up[i].reshape(256, cols).T

    count = routes.shape[1]
    diagonal = lax.broadcasted_iota(jnp.int32, (count, count), 0) == lax.broadcasted_iota(
        jnp.int32, (count, count), 1
    )

    def as_column(row):
        return jnp.sum(jnp.where(diagonal, jnp.broadcast_to(row, (count, count)), 0.0), 1, keepdims=True)

    lane = lax.broadcasted_iota(jnp.int32, (8, 128), 1).astype(jnp.float32)
    packed = jnp.zeros((8, 128), jnp.float32)
    for k in range(routes.shape[0]):
        chosen = as_column(routes[k : k + 1, :].astype(jnp.float32))
        amount = as_column(weights[k : k + 1, :])
        for g in range(count // 8):
            packed += jnp.where(lane == chosen[8 * g : 8 * g + 8] + 16.0 * g, amount[8 * g : 8 * g + 8], 0.0)
    coef[0, z] = packed
    for k in (1, 2, 3):
        send(coef.at[0, z], coef.at[0, z], cf_send.at[k], cf_recv.at[z], z_peer(k))

    for c in loads[:2]:
        c.wait()
    turn_tiles(0, 3)
    pass_column(0)
    send_z(1)
    turn_tiles(3, 6)
    pass_diagonal(0)
    turn_tiles(6, 8)
    pass_column(1)
    send_z(2)
    for k in (1, 2, 3):
        from_z = (z + k) % 4
        arrived(coef.at[0, from_z], cf_recv.at[from_z])
    send(coef.at[0], coef.at[1], cf_send.at[4], cf_recv.at[4], x_peer)
    send(coef.at[0], coef.at[2], cf_send.at[5], cf_recv.at[5], y_peer)
    turn_tiles(8, tiles)

    def add_tile(v, i):
        x = tok[v].reshape(2 * half_rows, cols)
        sums = lax.dot_general(x, gate_up_t[i], NN, preferred_element_type=jnp.float32)
        gsend[v, i] = sums.astype(jnp.bfloat16).reshape(2, half_rows, 256)
        copy(gsend.at[v, i, 1 - n], grecv.at[v, i], g_send.at[v, i], g_recv.at[v, i], w, 1 - n).start()

    def hide_tile(v, i):
        arrived(grecv.at[v, i], g_recv.at[v, i])
        sums = gsend[v, i, n].astype(jnp.float32) + grecv[v, i].astype(jnp.float32)
        gate, up = sums[:, :128], sums[:, 128:]
        lanes = pl.ds(pl.multiple_of(i * 128, 128), 128)
        hid[v, n, :, lanes] = (gate / (1.0 + jnp.exp(-gate)) * up).astype(jnp.bfloat16)
        there = hid.at[v, n, :, lanes]
        copy(there, there, h_send.at[v, i], h_recv.at[v, i], w, 1 - n).start()

    def hidden_units(v, meanwhile):
        @pl.loop(0, LAG)
        def _(i):
            add_tile(v, i)

        @pl.loop(LAG, tiles)
        def _(i):
            add_tile(v, i)
            hide_tile(v, i - LAG)

        meanwhile()

        @pl.loop(tiles - LAG, tiles)
        def _(i):
            hide_tile(v, i)

    def outputs(v, h):
        column = scale[v, pl.ds(8 * h, 8)].reshape(half_rows, 128)[:, 0:1]

        @pl.loop(0, cols // 256)
        def _(i):
            lanes = pl.ds(pl.multiple_of(i * 256, 256), 256)
            acc = lax.dot_general(hid[v, h], down[:, lanes], NN, preferred_element_type=jnp.float32)
            part[v, pl.ds(8 * h, 8), :, lanes] = (acc * column).astype(jnp.bfloat16).reshape(8, rows, 256)

    def other_hidden(v):
        @pl.loop(0, tiles)
        def _(i):
            lanes = pl.ds(pl.multiple_of(i * 128, 128), 128)
            arrived(hid.at[v, 1 - n, :, lanes], h_recv.at[v, i])

    def send_half(v, h):
        peer = x_peer + h * (y_peer - x_peer)
        for low in (0, 1):
            at = 2 * h + low
            send(part.at[v, place(3, at)], back.at[v, 0, at], rs_send.at[v, 0, at], rs_recv.at[v, 0, at], peer)
        for low in (0, 1):
            at = 2 * h + low
            send(
                part.at[v, place(1 + h, at)], back.at[v, 1 + h, at],
                rs_send.at[v, 1 + h, at], rs_recv.at[v, 1 + h, at], peer,
            )

    def relay_sums(v):
        for low in (0, 1):
            for h in (0, 1):
                at = 2 * h + low
                arrived(back.at[v, 0, at], rs_recv.at[v, 0, at])
                mine = part[v, place(2 - h, at)].astype(jnp.float32)
                part[v, place(2 - h, at)] = (mine + back[v, 0, at].astype(jnp.float32)).astype(jnp.bfloat16)
                send(
                    part.at[v, place(2 - h, at)], back.at[v, 2 - h, at],
                    rs_send.at[v, 2 - h, at], rs_recv.at[v, 2 - h, at], y_peer if h == 0 else x_peer,
                )

    def column_sums(v):
        for k in (2, 1, 3, 0):
            at = (z + k) % 4
            arrived(back.at[v, 1, at], rs_recv.at[v, 1, at])
            arrived(back.at[v, 2, at], rs_recv.at[v, 2, at])
            total = part[v, place(0, at)].astype(jnp.float32)
            total += back[v, 1, at].astype(jnp.float32) + back[v, 2, at].astype(jnp.float32)
            if k == 0:
                zrecv[v, z] = total.astype(jnp.bfloat16)
            else:
                zsend[v, k] = total.astype(jnp.bfloat16)
                send(zsend.at[v, k], zrecv.at[v, z], z_send.at[v, k], z_recv.at[v, z], z_peer(k))

    def finish(v):
        for k in (1, 3, 2):
            at = (z + k) % 4
            arrived(zrecv.at[v, at], z_recv.at[v, at])
        total = zrecv[v, 0].astype(jnp.float32) + zrecv[v, 1].astype(jnp.float32)
        total += zrecv[v, 2].astype(jnp.float32) + zrecv[v, 3].astype(jnp.float32)
        out[pl.ds(v * rows, rows), :] = total.astype(jnp.bfloat16)

    def make_scale():
        arrived(coef.at[2], cf_recv.at[5])
        arrived(coef.at[3], cf_recv.at[6])
        lane = lax.broadcasted_iota(jnp.int32, (4, 8, 128), 2)
        for column in range(4):
            block = coef[column]
            for g in range(tokens.shape[0] // 8):
                mine = jnp.sum(jnp.where(lane == 16 * g + w, block, 0.0), 2, keepdims=True)
                mine = jnp.broadcast_to(mine, (4, 8, 128))
                for at in range(4):
                    scale[g * 8 // rows, place(column, at), g % (rows // 8)] = mine[at]

    def give(v):
        outputs(v, n)
        send_half(v, n)
        other_hidden(v)
        outputs(v, 1 - n)
        send_half(v, 1 - n)

    def between_0():
        arrived(coef.at[1], cf_recv.at[4])
        send(coef.at[1], coef.at[3], cf_send.at[6], cf_recv.at[6], y_peer)
        pass_diagonal(1)
        pass_column(2)
        send_z(3)

    def between_1():
        pass_diagonal(2)
        pass_column(3)
        relay_sums(0)

    def between_2():
        pass_diagonal(3)
        relay_sums(1)

    gather_rest(0)
    hidden_units(0, between_0)
    make_scale()
    loads[2].wait()
    give(0)

    gather_rest(1)
    hidden_units(1, between_1)
    give(1)

    gather_rest(2)
    hidden_units(2, between_2)
    column_sums(0)
    give(2)

    gather_rest(3)
    hidden_units(3, lambda: relay_sums(2))
    column_sums(1)
    give(3)

    column_sums(2)
    relay_sums(3)
    column_sums(3)
    for v in range(WAVES):
        finish(v)

    for c in sent:
        c.wait_send()
    for v in range(WAVES):

        @pl.loop(0, tiles)
        def _(i):
            lanes = pl.ds(pl.multiple_of(i * 128, 128), 128)
            there = hid.at[v, n, :, lanes]
            copy(gsend.at[v, i, 1 - n], grecv.at[v, i], g_send.at[v, i], g_recv.at[v, i], w, 1 - n).wait_send()
            copy(there, there, h_send.at[v, i], h_recv.at[v, i], w, 1 - n).wait_send()


def gather_plan(tokens, routes, route_weight, w_gate, w_up, w_down):
    count = tokens.shape[0]
    hidden, cols = w_gate.shape[1:]
    tiles = hidden // 128
    rows = count // WAVES
    half = 8 * rows
    bf16, f32 = jnp.bfloat16, jnp.float32
    dma = pltpu.SemaphoreType.DMA
    vmem = pl.BlockSpec(memory_space=pltpu.VMEM)
    anywhere = pl.BlockSpec(memory_space=pl.ANY)
    flops = 2 * 16 * count * hidden * cols * 3
    return pl.pallas_call(
        kernel,
        out_shape=jax.ShapeDtypeStruct((count, cols), bf16),
        in_specs=[anywhere] * 6,
        out_specs=vmem,
        scratch_shapes=[
            pltpu.VMEM((route_weight.shape[1], count), jnp.int32),
            pltpu.VMEM((route_weight.shape[1], count), f32),
            pltpu.VMEM((WAVES, 16, rows, cols), bf16),
            pltpu.VMEM((tiles, 2, 128, cols), bf16),
            pltpu.VMEM((tiles, cols, 256), bf16),
            pltpu.VMEM((hidden, cols), bf16),
            pltpu.VMEM((4, 4, 8, 128), f32),
            pltpu.VMEM((WAVES, 16, rows // 8, 8, 128), f32),
            pltpu.VMEM((WAVES, tiles, 2, half, 256), bf16),
            pltpu.VMEM((WAVES, tiles, half, 256), bf16),
            pltpu.VMEM((WAVES, 2, half, hidden), bf16),
            pltpu.VMEM((WAVES, 16, rows, cols), bf16),
            pltpu.VMEM((WAVES, 3, 4, rows, cols), bf16),
            pltpu.VMEM((WAVES, 4, rows, cols), bf16),
            pltpu.VMEM((WAVES, 4, rows, cols), bf16),
            dma((5,)), dma((WAVES,)),
            dma((WAVES, 4, 4)), dma((WAVES, 4, 4)),
            dma((7,)), dma((7,)),
            dma((WAVES, tiles)), dma((WAVES, tiles)),
            dma((WAVES, tiles)), dma((WAVES, tiles)),
            dma((WAVES, 3, 4)), dma((WAVES, 3, 4)),
            dma((WAVES, 4)), dma((WAVES, 4)),
        ],
        compiler_params=pltpu.CompilerParams(
            collective_id=0, has_side_effects=True, vmem_limit_bytes=64 * 1024 * 1024 - 128 * 1024
        ),
        cost_estimate=pl.CostEstimate(
            flops=flops, bytes_accessed=3 * hidden * cols * 2, transcendentals=8 * count * hidden
        ),
    )(
        tokens, routes.T, route_weight.T,
        w_gate.reshape(tiles, 128, cols), w_up.reshape(tiles, 128, cols), w_down[0],
    )


def solution(mesh):
    chips = mesh.shape["wide"] == 16 and mesh.shape["narrow"] == 2
    return jax.shard_map(
        gather_plan if chips else slots_plan,
        mesh=mesh,
        in_specs=(
            P("wide", None),
            P("wide", None),
            P("wide", None),
            P("wide", None, "narrow"),
            P("wide", None, "narrow"),
            P("wide", None, "narrow"),
        ),
        out_specs=P("wide", "narrow"),
        check_vma=False,
    )
```

```python
import jax
import jax.numpy as jnp
from jax import lax
from jax.experimental import pallas as pl
from jax.experimental.pallas import tpu as pltpu
from jax.sharding import PartitionSpec as P


def slot_numbers(routes, experts):
    flat_routes = routes.reshape(-1)
    onehot = (flat_routes[:, None] == jnp.arange(experts, dtype=jnp.int32)[None, :]).astype(
        jnp.int32
    )
    before = jnp.cumsum(onehot, 0) - onehot
    return jnp.sum(before * onehot, 1).reshape(routes.shape)


def slots_plan(tokens, routes, route_weight, w_gate, w_up, w_down):
    tok_count = tokens.shape[0]
    model_width = tokens.shape[1]
    wide_count = lax.axis_size("wide")
    narrow_count = lax.axis_size("narrow")
    local_experts = w_gate.shape[0]
    experts = local_experts * wide_count
    capacity = max(2, (11 * tok_count + experts - 1) // experts)
    column_width = model_width // narrow_count
    slot_index = slot_numbers(routes, experts)
    target = routes * capacity + slot_index
    lane_ids = jnp.arange(experts * capacity, dtype=jnp.int32)
    picker = jnp.sum((lane_ids[:, None, None] == target[None, :, :]).astype(jnp.int32), 2).astype(
        jnp.bfloat16
    )
    columns = lax.dynamic_slice_in_dim(
        tokens, lax.axis_index("narrow") * column_width, column_width, 1
    )
    outgoing = jnp.dot(picker, columns, preferred_element_type=jnp.float32).astype(jnp.bfloat16)
    outgoing = outgoing.reshape(experts, capacity, column_width)
    received = lax.all_to_all(outgoing, "wide", split_axis=0, concat_axis=1, tiled=True)
    expert_rows = received[0]
    slot_total = expert_rows.shape[0]
    gate_matrix = w_gate[0]
    up_matrix = w_up[0]
    down_matrix = w_down[0]
    gate_term = jnp.einsum(
        "sc,fc->fs", expert_rows, gate_matrix, preferred_element_type=jnp.float32
    )
    up_term = jnp.einsum("sc,fc->fs", expert_rows, up_matrix, preferred_element_type=jnp.float32)
    sums = lax.psum_scatter(
        jnp.concatenate([gate_term, up_term], 1).astype(jnp.bfloat16),
        "narrow",
        scatter_dimension=0,
        tiled=True,
    ).astype(jnp.float32)
    hidden = (jax.nn.silu(sums[:, :slot_total]) * sums[:, slot_total:]).astype(jnp.bfloat16)
    produced = jnp.einsum(
        "fs,fc->sc",
        lax.all_gather(hidden, "narrow", axis=0, tiled=True),
        down_matrix,
        preferred_element_type=jnp.float32,
    )
    expert_out = produced.astype(jnp.bfloat16).reshape(local_experts, slot_total, column_width)
    returned = lax.all_to_all(expert_out, "wide", split_axis=1, concat_axis=0, tiled=True)
    flat_rows = returned.reshape(experts * capacity, column_width)
    picked = jnp.take(flat_rows, target, axis=0).astype(jnp.float32)
    combined = jnp.sum(picked * route_weight[:, :, None], 1)
    return combined.astype(jnp.bfloat16)


WAVES = 4
NN = (((1,), (0,)), ((), ()))


def place(column, z):
    return (z // 2) * 8 + column * 2 + z % 2


def kernel(
    tokens, routes_hbm, weights_hbm, gate_hbm, up_hbm, down_hbm, out,
    routes, weights, tok, gate_up, gate_up_t, down, coef, scale, gsend, grecv, hid, part, back, zsend, zrecv,
    load_sem, own_sem, ag_send, ag_recv, cf_send, cf_recv,
    g_send, g_recv, h_send, h_recv, rs_send, rs_recv, z_send, z_recv,
):
    w = lax.axis_index("wide")
    n = lax.axis_index("narrow")
    z = w // 4
    x_peer = w + 1 - 2 * (w % 2)
    y_peer = w + 2 - 4 * ((w // 2) % 2)
    tiles = gate_up.shape[0]
    rows = tok.shape[2]
    half_rows = 8 * rows
    cols = tok.shape[3]

    def copy(src, dst, send, recv, wide, narrow=n):
        return pltpu.make_async_remote_copy(
            src_ref=src, dst_ref=dst, send_sem=send, recv_sem=recv,
            device_id=(wide, narrow), device_id_type=pl.DeviceIdType.MESH,
        )

    def arrived(dst, recv, wide=x_peer):
        copy(dst, dst, recv, recv, wide).wait_recv()

    sent = []

    def send(src, dst, send_sem, recv_sem, wide, narrow=n):
        c = copy(src, dst, send_sem, recv_sem, wide, narrow)
        c.start()
        sent.append(c)

    def z_peer(k):
        return (w + 4 * k) % 16

    barrier = pltpu.get_barrier_semaphore()
    for wide, narrow in [(z_peer(k), n) for k in (1, 2, 3)] + [(x_peer, n), (y_peer, n), (w, 1 - n)]:
        pl.semaphore_signal(barrier, inc=1, device_id=(wide, narrow), device_id_type=pl.DeviceIdType.MESH)
    loads = [
        pltpu.make_async_copy(gate_hbm, gate_up.at[:, 0], load_sem.at[0]),
        pltpu.make_async_copy(up_hbm, gate_up.at[:, 1], load_sem.at[1]),
        pltpu.make_async_copy(down_hbm, down, load_sem.at[2]),
        pltpu.make_async_copy(routes_hbm, routes, load_sem.at[3]),
        pltpu.make_async_copy(weights_hbm, weights, load_sem.at[4]),
    ]
    own_block = [tokens.at[pl.ds(v * rows, rows), pl.ds(pl.multiple_of(n * cols, cols), cols)] for v in range(WAVES)]
    own_copy = [
        pltpu.make_async_copy(own_block[v], tok.at[v, place(0, z)], own_sem.at[v]) for v in range(WAVES)
    ]
    for c in loads[3:]:
        c.start()
    pl.semaphore_wait(barrier, 6)

    def send_z(v):
        for k in (1, 3, 2):
            send(own_block[v], tok.at[v, place(0, z)], ag_send.at[v, 0, k], ag_recv.at[v, 0, z], z_peer(k))

    def send_xy(v, src, from_z):
        send(src, tok.at[v, place(1, from_z)], ag_send.at[v, 1, from_z], ag_recv.at[v, 1, from_z], x_peer)
        send(src, tok.at[v, place(2, from_z)], ag_send.at[v, 2, from_z], ag_recv.at[v, 2, from_z], y_peer)

    def pass_column(v):
        for k in (1, 3, 2):
            from_z = (z + k) % 4
            block = tok.at[v, place(0, from_z)]
            arrived(block, ag_recv.at[v, 0, from_z])
            send_xy(v, block, from_z)

    def pass_diagonal(v):
        for k in (0, 1, 3, 2):
            from_z = (z + k) % 4
            h = from_z // 2
            block = tok.at[v, place(1 + h, from_z)]
            arrived(block, ag_recv.at[v, 1 + h, from_z])
            send(
                block, tok.at[v, place(3, from_z)], ag_send.at[v, 3, from_z], ag_recv.at[v, 3, from_z],
                y_peer + h * (x_peer - y_peer),
            )

    def gather_rest(v):
        for low in (0, 1):
            for h in (0, 1):
                from_z = 2 * h + low
                arrived(tok.at[v, place(2 - h, from_z)], ag_recv.at[v, 2 - h, from_z])
                arrived(tok.at[v, place(3, from_z)], ag_recv.at[v, 3, from_z])
        own_copy[v].wait()

    send_z(0)
    for v in range(WAVES):
        send_xy(v, own_block[v], z)
    for c in own_copy + loads[:3]:
        c.start()
    for c in loads[3:]:
        c.wait()

    def turn_tiles(first, last):
        @pl.loop(first, last)
        def _(i):
            gate_up_t[i] = gate_up[i].reshape(256, cols).T

    count = routes.shape[1]
    diagonal = lax.broadcasted_iota(jnp.int32, (count, count), 0) == lax.broadcasted_iota(
        jnp.int32, (count, count), 1
    )

    def as_column(row):
        return jnp.sum(jnp.where(diagonal, jnp.broadcast_to(row, (count, count)), 0.0), 1, keepdims=True)

    lane = lax.broadcasted_iota(jnp.int32, (8, 128), 1).astype(jnp.float32)
    packed = jnp.zeros((8, 128), jnp.float32)
    for k in range(routes.shape[0]):
        chosen = as_column(routes[k : k + 1, :].astype(jnp.float32))
        amount = as_column(weights[k : k + 1, :])
        for g in range(count // 8):
            packed += jnp.where(lane == chosen[8 * g : 8 * g + 8] + 16.0 * g, amount[8 * g : 8 * g + 8], 0.0)
    coef[0, z] = packed
    for k in (1, 2, 3):
        send(coef.at[0, z], coef.at[0, z], cf_send.at[k], cf_recv.at[z], z_peer(k))

    for c in loads[:2]:
        c.wait()
    turn_tiles(0, 3)
    pass_column(0)
    send_z(1)
    turn_tiles(3, 6)
    pass_diagonal(0)
    turn_tiles(6, 8)
    pass_column(1)
    send_z(2)
    for k in (1, 2, 3):
        from_z = (z + k) % 4
        arrived(coef.at[0, from_z], cf_recv.at[from_z])
    send(coef.at[0], coef.at[1], cf_send.at[4], cf_recv.at[4], x_peer)
    send(coef.at[0], coef.at[2], cf_send.at[5], cf_recv.at[5], y_peer)
    turn_tiles(8, tiles)

    def step(v, later, earlier):
        x = tok[v].reshape(2 * half_rows, cols)
        for j in earlier:
            arrived(grecv.at[v, j], g_recv.at[v, j])
        sums = [lax.dot_general(x, gate_up_t[i], NN, preferred_element_type=jnp.float32) for i in later]
        hidden = []
        for j in earlier:
            total = gsend[v, j, n].astype(jnp.float32) + grecv[v, j].astype(jnp.float32)
            gate, up = total[:, :128], total[:, 128:]
            hidden.append((gate / (1.0 + jnp.exp(-gate)) * up).astype(jnp.bfloat16))
        for i, value in zip(later, sums):
            gsend[v, i] = value.astype(jnp.bfloat16).reshape(2, half_rows, 256)
        places = [hid.at[v, n, :, pl.ds(pl.multiple_of(j * 128, 128), 128)] for j in earlier]
        for there, value in zip(places, hidden):
            there[...] = value
        for i in later:
            copy(gsend.at[v, i, 1 - n], grecv.at[v, i], g_send.at[v, i], g_recv.at[v, i], w, 1 - n).start()
        for j, there in zip(earlier, places):
            copy(there, there, h_send.at[v, j], h_recv.at[v, j], w, 1 - n).start()

    def hidden_units(v, meanwhile):
        lead = 2 + tiles % 2
        step(v, range(lead), ())

        @pl.loop(0, (tiles - lead) // 2)
        def _(i):
            step(v, (2 * i + lead, 2 * i + lead + 1), (2 * i, 2 * i + 1))

        meanwhile()
        step(v, (), range(tiles - lead, tiles))

    def outputs(v, first, halves):
        column = scale[v, pl.ds(8 * first, 8 * halves)].reshape(halves * half_rows, 128)[:, 0:1]
        units = hid[v, pl.ds(first, halves)].reshape(halves * half_rows, hid.shape[3])

        @pl.loop(0, cols // 512)
        def _(i):
            lanes = pl.ds(pl.multiple_of(i * 512, 512), 512)
            acc = lax.dot_general(units, down[:, lanes], NN, preferred_element_type=jnp.float32)
            part[v, pl.ds(8 * first, 8 * halves), :, lanes] = (
                (acc * column).astype(jnp.bfloat16).reshape(8 * halves, rows, 512)
            )

    def other_hidden(v):
        @pl.loop(0, tiles)
        def _(i):
            lanes = pl.ds(pl.multiple_of(i * 128, 128), 128)
            arrived(hid.at[v, 1 - n, :, lanes], h_recv.at[v, i])

    def send_half(v, h):
        peer = x_peer + h * (y_peer - x_peer)
        for low in (0, 1):
            at = 2 * h + low
            send(part.at[v, place(3, at)], back.at[v, 0, at], rs_send.at[v, 0, at], rs_recv.at[v, 0, at], peer)
        for low in (0, 1):
            at = 2 * h + low
            send(
                part.at[v, place(1 + h, at)], back.at[v, 1 + h, at],
                rs_send.at[v, 1 + h, at], rs_recv.at[v, 1 + h, at], peer,
            )

    def relay_sums(v):
        for low in (0, 1):
            for h in (0, 1):
                at = 2 * h + low
                arrived(back.at[v, 0, at], rs_recv.at[v, 0, at])
                mine = part[v, place(2 - h, at)].astype(jnp.float32)
                part[v, place(2 - h, at)] = (mine + back[v, 0, at].astype(jnp.float32)).astype(jnp.bfloat16)
                send(
                    part.at[v, place(2 - h, at)], back.at[v, 2 - h, at],
                    rs_send.at[v, 2 - h, at], rs_recv.at[v, 2 - h, at], y_peer if h == 0 else x_peer,
                )

    def column_sums(v):
        for k in (2, 1, 3, 0):
            at = (z + k) % 4
            arrived(back.at[v, 1, at], rs_recv.at[v, 1, at])
            arrived(back.at[v, 2, at], rs_recv.at[v, 2, at])
            total = part[v, place(0, at)].astype(jnp.float32)
            total += back[v, 1, at].astype(jnp.float32) + back[v, 2, at].astype(jnp.float32)
            if k == 0:
                zrecv[v, z] = total.astype(jnp.bfloat16)
            else:
                zsend[v, k] = total.astype(jnp.bfloat16)
                send(zsend.at[v, k], zrecv.at[v, z], z_send.at[v, k], z_recv.at[v, z], z_peer(k))

    def finish(v):
        for k in (1, 3, 2):
            at = (z + k) % 4
            arrived(zrecv.at[v, at], z_recv.at[v, at])
        total = zrecv[v, 0].astype(jnp.float32) + zrecv[v, 1].astype(jnp.float32)
        total += zrecv[v, 2].astype(jnp.float32) + zrecv[v, 3].astype(jnp.float32)
        out[pl.ds(v * rows, rows), :] = total.astype(jnp.bfloat16)

    def make_scale():
        arrived(coef.at[2], cf_recv.at[5])
        arrived(coef.at[3], cf_recv.at[6])
        lane = lax.broadcasted_iota(jnp.int32, (4, 8, 128), 2)
        for column in range(4):
            block = coef[column]
            for g in range(tokens.shape[0] // 8):
                mine = jnp.sum(jnp.where(lane == 16 * g + w, block, 0.0), 2, keepdims=True)
                mine = jnp.broadcast_to(mine, (4, 8, 128))
                for at in range(4):
                    scale[g * 8 // rows, place(column, at), g % (rows // 8)] = mine[at]

    def give(v):
        other_hidden(v)
        outputs(v, 0, 2)
        send_half(v, n)
        send_half(v, 1 - n)

    def between_0():
        arrived(coef.at[1], cf_recv.at[4])
        send(coef.at[1], coef.at[3], cf_send.at[6], cf_recv.at[6], y_peer)
        pass_diagonal(1)
        pass_column(2)
        send_z(3)

    def between_1():
        pass_diagonal(2)
        pass_column(3)
        relay_sums(0)

    def between_2():
        pass_diagonal(3)
        relay_sums(1)

    gather_rest(0)
    hidden_units(0, between_0)
    make_scale()
    loads[2].wait()
    give(0)

    gather_rest(1)
    hidden_units(1, between_1)
    give(1)

    gather_rest(2)
    hidden_units(2, between_2)
    column_sums(0)
    give(2)

    gather_rest(3)
    hidden_units(3, lambda: relay_sums(2))
    column_sums(1)
    outputs(3, n, 1)
    send_half(3, n)
    other_hidden(3)
    outputs(3, 1 - n, 1)
    send_half(3, 1 - n)

    column_sums(2)
    relay_sums(3)
    column_sums(3)
    for v in range(WAVES):
        finish(v)

    for c in sent:
        c.wait_send()
    for v in range(WAVES):

        @pl.loop(0, tiles)
        def _(i):
            lanes = pl.ds(pl.multiple_of(i * 128, 128), 128)
            there = hid.at[v, n, :, lanes]
            copy(gsend.at[v, i, 1 - n], grecv.at[v, i], g_send.at[v, i], g_recv.at[v, i], w, 1 - n).wait_send()
            copy(there, there, h_send.at[v, i], h_recv.at[v, i], w, 1 - n).wait_send()


def gather_plan(tokens, routes, route_weight, w_gate, w_up, w_down):
    count = tokens.shape[0]
    hidden, cols = w_gate.shape[1:]
    tiles = hidden // 128
    rows = count // WAVES
    half = 8 * rows
    bf16, f32 = jnp.bfloat16, jnp.float32
    dma = pltpu.SemaphoreType.DMA
    vmem = pl.BlockSpec(memory_space=pltpu.VMEM)
    anywhere = pl.BlockSpec(memory_space=pl.ANY)
    flops = 2 * 16 * count * hidden * cols * 3
    return pl.pallas_call(
        kernel,
        out_shape=jax.ShapeDtypeStruct((count, cols), bf16),
        in_specs=[anywhere] * 6,
        out_specs=vmem,
        scratch_shapes=[
            pltpu.VMEM((route_weight.shape[1], count), jnp.int32),
            pltpu.VMEM((route_weight.shape[1], count), f32),
            pltpu.VMEM((WAVES, 16, rows, cols), bf16),
            pltpu.VMEM((tiles, 2, 128, cols), bf16),
            pltpu.VMEM((tiles, cols, 256), bf16),
            pltpu.VMEM((hidden, cols), bf16),
            pltpu.VMEM((4, 4, 8, 128), f32),
            pltpu.VMEM((WAVES, 16, rows // 8, 8, 128), f32),
            pltpu.VMEM((WAVES, tiles, 2, half, 256), bf16),
            pltpu.VMEM((WAVES, tiles, half, 256), bf16),
            pltpu.VMEM((WAVES, 2, half, hidden), bf16),
            pltpu.VMEM((WAVES, 16, rows, cols), bf16),
            pltpu.VMEM((WAVES, 3, 4, rows, cols), bf16),
            pltpu.VMEM((WAVES, 4, rows, cols), bf16),
            pltpu.VMEM((WAVES, 4, rows, cols), bf16),
            dma((5,)), dma((WAVES,)),
            dma((WAVES, 4, 4)), dma((WAVES, 4, 4)),
            dma((7,)), dma((7,)),
            dma((WAVES, tiles)), dma((WAVES, tiles)),
            dma((WAVES, tiles)), dma((WAVES, tiles)),
            dma((WAVES, 3, 4)), dma((WAVES, 3, 4)),
            dma((WAVES, 4)), dma((WAVES, 4)),
        ],
        compiler_params=pltpu.CompilerParams(
            collective_id=0, has_side_effects=True, vmem_limit_bytes=64 * 1024 * 1024 - 128 * 1024
        ),
        cost_estimate=pl.CostEstimate(
            flops=flops, bytes_accessed=3 * hidden * cols * 2, transcendentals=8 * count * hidden
        ),
    )(
        tokens, routes.T, route_weight.T,
        w_gate.reshape(tiles, 128, cols), w_up.reshape(tiles, 128, cols), w_down[0],
    )


def solution(mesh):
    chips = mesh.shape["wide"] == 16 and mesh.shape["narrow"] == 2
    return jax.shard_map(
        gather_plan if chips else slots_plan,
        mesh=mesh,
        in_specs=(
            P("wide", None),
            P("wide", None),
            P("wide", None),
            P("wide", None, "narrow"),
            P("wide", None, "narrow"),
            P("wide", None, "narrow"),
        ),
        out_specs=P("wide", "narrow"),
        check_vma=False,
    )
```

```python
import jax
import jax.numpy as jnp
from jax import lax
from jax.experimental import pallas as pl
from jax.experimental.pallas import tpu as pltpu
from jax.sharding import PartitionSpec as P


def slot_numbers(routes, experts):
    flat_routes = routes.reshape(-1)
    onehot = (flat_routes[:, None] == jnp.arange(experts, dtype=jnp.int32)[None, :]).astype(
        jnp.int32
    )
    before = jnp.cumsum(onehot, 0) - onehot
    return jnp.sum(before * onehot, 1).reshape(routes.shape)


def slots_plan(tokens, routes, route_weight, w_gate, w_up, w_down):
    tok_count = tokens.shape[0]
    model_width = tokens.shape[1]
    wide_count = lax.axis_size("wide")
    narrow_count = lax.axis_size("narrow")
    local_experts = w_gate.shape[0]
    experts = local_experts * wide_count
    capacity = max(2, (11 * tok_count + experts - 1) // experts)
    column_width = model_width // narrow_count
    slot_index = slot_numbers(routes, experts)
    target = routes * capacity + slot_index
    lane_ids = jnp.arange(experts * capacity, dtype=jnp.int32)
    picker = jnp.sum((lane_ids[:, None, None] == target[None, :, :]).astype(jnp.int32), 2).astype(
        jnp.bfloat16
    )
    columns = lax.dynamic_slice_in_dim(
        tokens, lax.axis_index("narrow") * column_width, column_width, 1
    )
    outgoing = jnp.dot(picker, columns, preferred_element_type=jnp.float32).astype(jnp.bfloat16)
    outgoing = outgoing.reshape(experts, capacity, column_width)
    received = lax.all_to_all(outgoing, "wide", split_axis=0, concat_axis=1, tiled=True)
    expert_rows = received[0]
    slot_total = expert_rows.shape[0]
    gate_matrix = w_gate[0]
    up_matrix = w_up[0]
    down_matrix = w_down[0]
    gate_term = jnp.einsum(
        "sc,fc->fs", expert_rows, gate_matrix, preferred_element_type=jnp.float32
    )
    up_term = jnp.einsum("sc,fc->fs", expert_rows, up_matrix, preferred_element_type=jnp.float32)
    sums = lax.psum_scatter(
        jnp.concatenate([gate_term, up_term], 1).astype(jnp.bfloat16),
        "narrow",
        scatter_dimension=0,
        tiled=True,
    ).astype(jnp.float32)
    hidden = (jax.nn.silu(sums[:, :slot_total]) * sums[:, slot_total:]).astype(jnp.bfloat16)
    produced = jnp.einsum(
        "fs,fc->sc",
        lax.all_gather(hidden, "narrow", axis=0, tiled=True),
        down_matrix,
        preferred_element_type=jnp.float32,
    )
    expert_out = produced.astype(jnp.bfloat16).reshape(local_experts, slot_total, column_width)
    returned = lax.all_to_all(expert_out, "wide", split_axis=1, concat_axis=0, tiled=True)
    flat_rows = returned.reshape(experts * capacity, column_width)
    picked = jnp.take(flat_rows, target, axis=0).astype(jnp.float32)
    combined = jnp.sum(picked * route_weight[:, :, None], 1)
    return combined.astype(jnp.bfloat16)


WAVES = 4
NN = (((1,), (0,)), ((), ()))


def place(column, z):
    return (z // 2) * 8 + column * 2 + z % 2


def kernel(
    tokens, routes_hbm, weights_hbm, gate_hbm, up_hbm, down_hbm, out,
    routes, weights, tok, gate_up, gate_up_t, down, coef, scale, gsend, grecv, hid, part, back, zsend, zrecv,
    load_sem, own_sem, ag_send, ag_recv, cf_send, cf_recv,
    g_send, g_recv, h_send, h_recv, rs_send, rs_recv, z_send, z_recv,
):
    w = lax.axis_index("wide")
    n = lax.axis_index("narrow")
    z = w // 4
    x_peer = w + 1 - 2 * (w % 2)
    y_peer = w + 2 - 4 * ((w // 2) % 2)
    tiles = gate_up.shape[0]
    rows = tok.shape[2]
    half_rows = 8 * rows
    cols = tok.shape[3]

    def copy(src, dst, send, recv, wide, narrow=n):
        return pltpu.make_async_remote_copy(
            src_ref=src, dst_ref=dst, send_sem=send, recv_sem=recv,
            device_id=(wide, narrow), device_id_type=pl.DeviceIdType.MESH,
        )

    def arrived(dst, recv, wide=x_peer):
        copy(dst, dst, recv, recv, wide).wait_recv()

    sent = []

    def send(src, dst, send_sem, recv_sem, wide, narrow=n):
        c = copy(src, dst, send_sem, recv_sem, wide, narrow)
        c.start()
        sent.append(c)

    def z_peer(k):
        return (w + 4 * k) % 16

    barrier = pltpu.get_barrier_semaphore()
    for wide, narrow in [(z_peer(k), n) for k in (1, 2, 3)] + [(x_peer, n), (y_peer, n), (w, 1 - n)]:
        pl.semaphore_signal(barrier, inc=1, device_id=(wide, narrow), device_id_type=pl.DeviceIdType.MESH)
    loads = [
        pltpu.make_async_copy(gate_hbm, gate_up.at[:, 0], load_sem.at[0]),
        pltpu.make_async_copy(up_hbm, gate_up.at[:, 1], load_sem.at[1]),
        pltpu.make_async_copy(down_hbm, down, load_sem.at[2]),
        pltpu.make_async_copy(routes_hbm, routes, load_sem.at[3]),
        pltpu.make_async_copy(weights_hbm, weights, load_sem.at[4]),
    ]
    own_block = [tokens.at[pl.ds(v * rows, rows), pl.ds(pl.multiple_of(n * cols, cols), cols)] for v in range(WAVES)]
    own_copy = [
        pltpu.make_async_copy(own_block[v], tok.at[v, place(0, z)], own_sem.at[v]) for v in range(WAVES)
    ]
    for c in loads[3:]:
        c.start()
    pl.semaphore_wait(barrier, 6)

    def send_z(v):
        for k in (1, 3, 2):
            send(own_block[v], tok.at[v, place(0, z)], ag_send.at[v, 0, k], ag_recv.at[v, 0, z], z_peer(k))

    def send_xy(v, src, from_z):
        send(src, tok.at[v, place(1, from_z)], ag_send.at[v, 1, from_z], ag_recv.at[v, 1, from_z], x_peer)
        send(src, tok.at[v, place(2, from_z)], ag_send.at[v, 2, from_z], ag_recv.at[v, 2, from_z], y_peer)

    def pass_column(v):
        for k in (1, 3, 2):
            from_z = (z + k) % 4
            block = tok.at[v, place(0, from_z)]
            arrived(block, ag_recv.at[v, 0, from_z])
            send_xy(v, block, from_z)

    def pass_diagonal(v):
        for k in (0, 1, 3, 2):
            from_z = (z + k) % 4
            h = from_z // 2
            block = tok.at[v, place(1 + h, from_z)]
            arrived(block, ag_recv.at[v, 1 + h, from_z])
            send(
                block, tok.at[v, place(3, from_z)], ag_send.at[v, 3, from_z], ag_recv.at[v, 3, from_z],
                y_peer + h * (x_peer - y_peer),
            )

    def gather_rest(v):
        for low in (0, 1):
            for h in (0, 1):
                from_z = 2 * h + low
                arrived(tok.at[v, place(2 - h, from_z)], ag_recv.at[v, 2 - h, from_z])
                arrived(tok.at[v, place(3, from_z)], ag_recv.at[v, 3, from_z])
        own_copy[v].wait()

    send_z(0)
    for v in range(WAVES):
        send_xy(v, own_block[v], z)
    for c in own_copy + loads[:3]:
        c.start()
    for c in loads[3:]:
        c.wait()

    def turn_tiles(first, last):
        @pl.loop(first, last)
        def _(i):
            gate_up_t[i] = gate_up[i].reshape(256, cols).T

    count = routes.shape[1]
    diagonal = lax.broadcasted_iota(jnp.int32, (count, count), 0) == lax.broadcasted_iota(
        jnp.int32, (count, count), 1
    )

    def as_column(row):
        return jnp.sum(jnp.where(diagonal, jnp.broadcast_to(row, (count, count)), 0.0), 1, keepdims=True)

    lane = lax.broadcasted_iota(jnp.int32, (8, 128), 1).astype(jnp.float32)
    packed = jnp.zeros((8, 128), jnp.float32)
    for k in range(routes.shape[0]):
        chosen = as_column(routes[k : k + 1, :].astype(jnp.float32))
        amount = as_column(weights[k : k + 1, :])
        for g in range(count // 8):
            packed += jnp.where(lane == chosen[8 * g : 8 * g + 8] + 16.0 * g, amount[8 * g : 8 * g + 8], 0.0)
    coef[0, z] = packed
    for k in (1, 2, 3):
        send(coef.at[0, z], coef.at[0, z], cf_send.at[k], cf_recv.at[z], z_peer(k))

    for c in loads[:2]:
        c.wait()
    turn_tiles(0, 3)
    pass_column(0)
    send_z(1)
    turn_tiles(3, 6)
    pass_diagonal(0)
    turn_tiles(6, 8)
    pass_column(1)
    send_z(2)
    for k in (1, 2, 3):
        from_z = (z + k) % 4
        arrived(coef.at[0, from_z], cf_recv.at[from_z])
    send(coef.at[0], coef.at[1], cf_send.at[4], cf_recv.at[4], x_peer)
    send(coef.at[0], coef.at[2], cf_send.at[5], cf_recv.at[5], y_peer)
    turn_tiles(8, tiles)

    def half(v, h):
        return tok[v, pl.ds(8 * h, 8)].reshape(half_rows, cols)

    def partner_sums(v):
        @pl.loop(0, tiles)
        def _(i):
            sums = lax.dot_general(half(v, 1 - n), gate_up_t[i], NN, preferred_element_type=jnp.float32)
            gsend[v, i] = sums.astype(jnp.bfloat16)
            copy(gsend.at[v, i], grecv.at[v, i], g_send.at[v, i], g_recv.at[v, i], w, 1 - n).start()

    def own_hidden(v):
        @pl.loop(0, tiles)
        def _(i):
            sums = lax.dot_general(half(v, n), gate_up_t[i], NN, preferred_element_type=jnp.float32)
            arrived(grecv.at[v, i], g_recv.at[v, i])
            sums += grecv[v, i].astype(jnp.float32)
            gate, up = sums[:, :128], sums[:, 128:]
            there = hid.at[v, n, :, pl.ds(pl.multiple_of(i * 128, 128), 128)]
            there[...] = (gate / (1.0 + jnp.exp(-gate)) * up).astype(jnp.bfloat16)
            copy(there, there, h_send.at[v, i], h_recv.at[v, i], w, 1 - n).start()

    def hidden_units(v, meanwhile):
        partner_sums(v)
        meanwhile()
        own_hidden(v)

    def outputs(v, h):
        column = scale[v, pl.ds(8 * h, 8)].reshape(half_rows, 128)[:, 0:1]

        @pl.loop(0, cols // 256)
        def _(i):
            lanes = pl.ds(pl.multiple_of(i * 256, 256), 256)
            acc = lax.dot_general(hid[v, h], down[:, lanes], NN, preferred_element_type=jnp.float32)
            part[v, pl.ds(8 * h, 8), :, lanes] = (acc * column).astype(jnp.bfloat16).reshape(8, rows, 256)

    def other_hidden(v):
        @pl.loop(0, tiles)
        def _(i):
            lanes = pl.ds(pl.multiple_of(i * 128, 128), 128)
            arrived(hid.at[v, 1 - n, :, lanes], h_recv.at[v, i])

    def send_half(v, h):
        peer = x_peer + h * (y_peer - x_peer)
        for low in (0, 1):
            at = 2 * h + low
            send(part.at[v, place(3, at)], back.at[v, 0, at], rs_send.at[v, 0, at], rs_recv.at[v, 0, at], peer)
        for low in (0, 1):
            at = 2 * h + low
            send(
                part.at[v, place(1 + h, at)], back.at[v, 1 + h, at],
                rs_send.at[v, 1 + h, at], rs_recv.at[v, 1 + h, at], peer,
            )

    def relay_sums(v):
        for low in (0, 1):
            for h in (0, 1):
                at = 2 * h + low
                arrived(back.at[v, 0, at], rs_recv.at[v, 0, at])
                mine = part[v, place(2 - h, at)].astype(jnp.float32)
                part[v, place(2 - h, at)] = (mine + back[v, 0, at].astype(jnp.float32)).astype(jnp.bfloat16)
                send(
                    part.at[v, place(2 - h, at)], back.at[v, 2 - h, at],
                    rs_send.at[v, 2 - h, at], rs_recv.at[v, 2 - h, at], y_peer if h == 0 else x_peer,
                )

    def column_sums(v):
        for k in (2, 1, 3, 0):
            at = (z + k) % 4
            arrived(back.at[v, 1, at], rs_recv.at[v, 1, at])
            arrived(back.at[v, 2, at], rs_recv.at[v, 2, at])
            total = part[v, place(0, at)].astype(jnp.float32)
            total += back[v, 1, at].astype(jnp.float32) + back[v, 2, at].astype(jnp.float32)
            if k == 0:
                zrecv[v, z] = total.astype(jnp.bfloat16)
            else:
                zsend[v, k] = total.astype(jnp.bfloat16)
                send(zsend.at[v, k], zrecv.at[v, z], z_send.at[v, k], z_recv.at[v, z], z_peer(k))

    def finish(v):
        for k in (1, 3, 2):
            at = (z + k) % 4
            arrived(zrecv.at[v, at], z_recv.at[v, at])
        total = zrecv[v, 0].astype(jnp.float32) + zrecv[v, 1].astype(jnp.float32)
        total += zrecv[v, 2].astype(jnp.float32) + zrecv[v, 3].astype(jnp.float32)
        out[pl.ds(v * rows, rows), :] = total.astype(jnp.bfloat16)

    def make_scale():
        arrived(coef.at[2], cf_recv.at[5])
        arrived(coef.at[3], cf_recv.at[6])
        lane = lax.broadcasted_iota(jnp.int32, (4, 8, 128), 2)
        for column in range(4):
            block = coef[column]
            for g in range(tokens.shape[0] // 8):
                mine = jnp.sum(jnp.where(lane == 16 * g + w, block, 0.0), 2, keepdims=True)
                mine = jnp.broadcast_to(mine, (4, 8, 128))
                for at in range(4):
                    scale[g * 8 // rows, place(column, at), g % (rows // 8)] = mine[at]

    def give(v):
        outputs(v, n)
        send_half(v, n)
        other_hidden(v)
        outputs(v, 1 - n)
        send_half(v, 1 - n)

    def between_0():
        arrived(coef.at[1], cf_recv.at[4])
        send(coef.at[1], coef.at[3], cf_send.at[6], cf_recv.at[6], y_peer)
        pass_diagonal(1)
        pass_column(2)
        send_z(3)

    def between_1():
        pass_diagonal(2)
        pass_column(3)
        relay_sums(0)

    def between_2():
        pass_diagonal(3)
        relay_sums(1)

    gather_rest(0)
    hidden_units(0, between_0)
    make_scale()
    loads[2].wait()
    give(0)

    gather_rest(1)
    hidden_units(1, between_1)
    give(1)

    gather_rest(2)
    hidden_units(2, between_2)
    column_sums(0)
    give(2)

    gather_rest(3)
    hidden_units(3, lambda: relay_sums(2))
    column_sums(1)
    give(3)

    column_sums(2)
    relay_sums(3)
    column_sums(3)
    for v in range(WAVES):
        finish(v)

    for c in sent:
        c.wait_send()
    for v in range(WAVES):

        @pl.loop(0, tiles)
        def _(i):
            lanes = pl.ds(pl.multiple_of(i * 128, 128), 128)
            there = hid.at[v, n, :, lanes]
            copy(gsend.at[v, i], grecv.at[v, i], g_send.at[v, i], g_recv.at[v, i], w, 1 - n).wait_send()
            copy(there, there, h_send.at[v, i], h_recv.at[v, i], w, 1 - n).wait_send()


def gather_plan(tokens, routes, route_weight, w_gate, w_up, w_down):
    count = tokens.shape[0]
    hidden, cols = w_gate.shape[1:]
    tiles = hidden // 128
    rows = count // WAVES
    half = 8 * rows
    bf16, f32 = jnp.bfloat16, jnp.float32
    dma = pltpu.SemaphoreType.DMA
    vmem = pl.BlockSpec(memory_space=pltpu.VMEM)
    anywhere = pl.BlockSpec(memory_space=pl.ANY)
    flops = 2 * 16 * count * hidden * cols * 3
    return pl.pallas_call(
        kernel,
        out_shape=jax.ShapeDtypeStruct((count, cols), bf16),
        in_specs=[anywhere] * 6,
        out_specs=vmem,
        scratch_shapes=[
            pltpu.VMEM((route_weight.shape[1], count), jnp.int32),
            pltpu.VMEM((route_weight.shape[1], count), f32),
            pltpu.VMEM((WAVES, 16, rows, cols), bf16),
            pltpu.VMEM((tiles, 2, 128, cols), bf16),
            pltpu.VMEM((tiles, cols, 256), bf16),
            pltpu.VMEM((hidden, cols), bf16),
            pltpu.VMEM((4, 4, 8, 128), f32),
            pltpu.VMEM((WAVES, 16, rows // 8, 8, 128), f32),
            pltpu.VMEM((WAVES, tiles, half, 256), bf16),
            pltpu.VMEM((WAVES, tiles, half, 256), bf16),
            pltpu.VMEM((WAVES, 2, half, hidden), bf16),
            pltpu.VMEM((WAVES, 16, rows, cols), bf16),
            pltpu.VMEM((WAVES, 3, 4, rows, cols), bf16),
            pltpu.VMEM((WAVES, 4, rows, cols), bf16),
            pltpu.VMEM((WAVES, 4, rows, cols), bf16),
            dma((5,)), dma((WAVES,)),
            dma((WAVES, 4, 4)), dma((WAVES, 4, 4)),
            dma((7,)), dma((7,)),
            dma((WAVES, tiles)), dma((WAVES, tiles)),
            dma((WAVES, tiles)), dma((WAVES, tiles)),
            dma((WAVES, 3, 4)), dma((WAVES, 3, 4)),
            dma((WAVES, 4)), dma((WAVES, 4)),
        ],
        compiler_params=pltpu.CompilerParams(
            collective_id=0, has_side_effects=True, vmem_limit_bytes=64 * 1024 * 1024 - 128 * 1024
        ),
        cost_estimate=pl.CostEstimate(
            flops=flops, bytes_accessed=3 * hidden * cols * 2, transcendentals=8 * count * hidden
        ),
    )(
        tokens, routes.T, route_weight.T,
        w_gate.reshape(tiles, 128, cols), w_up.reshape(tiles, 128, cols), w_down[0],
    )


def solution(mesh):
    chips = mesh.shape["wide"] == 16 and mesh.shape["narrow"] == 2
    return jax.shard_map(
        gather_plan if chips else slots_plan,
        mesh=mesh,
        in_specs=(
            P("wide", None),
            P("wide", None),
            P("wide", None),
            P("wide", None, "narrow"),
            P("wide", None, "narrow"),
            P("wide", None, "narrow"),
        ),
        out_specs=P("wide", "narrow"),
        check_vma=False,
    )
```

```python
import jax
import jax.numpy as jnp
from jax import lax
from jax.experimental import pallas as pl
from jax.experimental.pallas import tpu as pltpu
from jax.sharding import PartitionSpec as P


def slot_numbers(routes, experts):
    flat_routes = routes.reshape(-1)
    onehot = (flat_routes[:, None] == jnp.arange(experts, dtype=jnp.int32)[None, :]).astype(
        jnp.int32
    )
    before = jnp.cumsum(onehot, 0) - onehot
    return jnp.sum(before * onehot, 1).reshape(routes.shape)


def slots_plan(tokens, routes, route_weight, w_gate, w_up, w_down):
    tok_count = tokens.shape[0]
    model_width = tokens.shape[1]
    wide_count = lax.axis_size("wide")
    narrow_count = lax.axis_size("narrow")
    local_experts = w_gate.shape[0]
    experts = local_experts * wide_count
    capacity = max(2, (11 * tok_count + experts - 1) // experts)
    column_width = model_width // narrow_count
    slot_index = slot_numbers(routes, experts)
    target = routes * capacity + slot_index
    lane_ids = jnp.arange(experts * capacity, dtype=jnp.int32)
    picker = jnp.sum((lane_ids[:, None, None] == target[None, :, :]).astype(jnp.int32), 2).astype(
        jnp.bfloat16
    )
    columns = lax.dynamic_slice_in_dim(
        tokens, lax.axis_index("narrow") * column_width, column_width, 1
    )
    outgoing = jnp.dot(picker, columns, preferred_element_type=jnp.float32).astype(jnp.bfloat16)
    outgoing = outgoing.reshape(experts, capacity, column_width)
    received = lax.all_to_all(outgoing, "wide", split_axis=0, concat_axis=1, tiled=True)
    expert_rows = received[0]
    slot_total = expert_rows.shape[0]
    gate_matrix = w_gate[0]
    up_matrix = w_up[0]
    down_matrix = w_down[0]
    gate_term = jnp.einsum(
        "sc,fc->fs", expert_rows, gate_matrix, preferred_element_type=jnp.float32
    )
    up_term = jnp.einsum("sc,fc->fs", expert_rows, up_matrix, preferred_element_type=jnp.float32)
    sums = lax.psum_scatter(
        jnp.concatenate([gate_term, up_term], 1).astype(jnp.bfloat16),
        "narrow",
        scatter_dimension=0,
        tiled=True,
    ).astype(jnp.float32)
    hidden = (jax.nn.silu(sums[:, :slot_total]) * sums[:, slot_total:]).astype(jnp.bfloat16)
    produced = jnp.einsum(
        "fs,fc->sc",
        lax.all_gather(hidden, "narrow", axis=0, tiled=True),
        down_matrix,
        preferred_element_type=jnp.float32,
    )
    expert_out = produced.astype(jnp.bfloat16).reshape(local_experts, slot_total, column_width)
    returned = lax.all_to_all(expert_out, "wide", split_axis=1, concat_axis=0, tiled=True)
    flat_rows = returned.reshape(experts * capacity, column_width)
    picked = jnp.take(flat_rows, target, axis=0).astype(jnp.float32)
    combined = jnp.sum(picked * route_weight[:, :, None], 1)
    return combined.astype(jnp.bfloat16)


WAVES = 4
LAG = 3
NN = (((1,), (0,)), ((), ()))


def place(column, z):
    return (z // 2) * 8 + column * 2 + z % 2


def kernel(
    tokens, routes_hbm, weights_hbm, gate_hbm, up_hbm, down_hbm, out,
    routes, weights, tok, gate_up, gate_up_t, down, coef, scale, gsend, grecv, hid, part, back, zsend, zrecv,
    load_sem, own_sem, ag_send, ag_recv, cf_send, cf_recv,
    g_send, g_recv, h_send, h_recv, rs_send, rs_recv, z_send, z_recv,
):
    w = lax.axis_index("wide")
    n = lax.axis_index("narrow")
    z = w // 4
    x_peer = w + 1 - 2 * (w % 2)
    y_peer = w + 2 - 4 * ((w // 2) % 2)
    tiles = gate_up.shape[0]
    rows = tok.shape[2]
    half_rows = 8 * rows
    cols = tok.shape[3]

    def copy(src, dst, send, recv, wide, narrow=n):
        return pltpu.make_async_remote_copy(
            src_ref=src, dst_ref=dst, send_sem=send, recv_sem=recv,
            device_id=(wide, narrow), device_id_type=pl.DeviceIdType.MESH,
        )

    def arrived(dst, recv, wide=x_peer):
        copy(dst, dst, recv, recv, wide).wait_recv()

    sent = []

    def send(src, dst, send_sem, recv_sem, wide, narrow=n):
        c = copy(src, dst, send_sem, recv_sem, wide, narrow)
        c.start()
        sent.append(c)

    def z_peer(k):
        return (w + 4 * k) % 16

    barrier = pltpu.get_barrier_semaphore()
    for wide, narrow in [(z_peer(k), n) for k in (1, 2, 3)] + [(x_peer, n), (y_peer, n), (w, 1 - n)]:
        pl.semaphore_signal(barrier, inc=1, device_id=(wide, narrow), device_id_type=pl.DeviceIdType.MESH)
    loads = [
        pltpu.make_async_copy(gate_hbm, gate_up.at[:, 0], load_sem.at[0]),
        pltpu.make_async_copy(up_hbm, gate_up.at[:, 1], load_sem.at[1]),
        pltpu.make_async_copy(down_hbm, down, load_sem.at[2]),
        pltpu.make_async_copy(routes_hbm, routes, load_sem.at[3]),
        pltpu.make_async_copy(weights_hbm, weights, load_sem.at[4]),
    ]
    own_block = [tokens.at[pl.ds(v * rows, rows), pl.ds(pl.multiple_of(n * cols, cols), cols)] for v in range(WAVES)]
    own_copy = [
        pltpu.make_async_copy(own_block[v], tok.at[v, place(0, z)], own_sem.at[v]) for v in range(WAVES)
    ]
    for c in loads[3:]:
        c.start()
    pl.semaphore_wait(barrier, 6)

    def send_z(v):
        for k in (1, 3, 2):
            send(own_block[v], tok.at[v, place(0, z)], ag_send.at[v, 0, k], ag_recv.at[v, 0, z], z_peer(k))

    def send_xy(v, src, from_z):
        send(src, tok.at[v, place(1, from_z)], ag_send.at[v, 1, from_z], ag_recv.at[v, 1, from_z], x_peer)
        send(src, tok.at[v, place(2, from_z)], ag_send.at[v, 2, from_z], ag_recv.at[v, 2, from_z], y_peer)

    def pass_column(v):
        for k in (1, 3, 2):
            from_z = (z + k) % 4
            block = tok.at[v, place(0, from_z)]
            arrived(block, ag_recv.at[v, 0, from_z])
            send_xy(v, block, from_z)

    def pass_diagonal(v):
        for k in (0, 1, 3, 2):
            from_z = (z + k) % 4
            h = from_z // 2
            block = tok.at[v, place(1 + h, from_z)]
            arrived(block, ag_recv.at[v, 1 + h, from_z])
            send(
                block, tok.at[v, place(3, from_z)], ag_send.at[v, 3, from_z], ag_recv.at[v, 3, from_z],
                y_peer + h * (x_peer - y_peer),
            )

    def gather_rest(v):
        for low in (0, 1):
            for h in (0, 1):
                from_z = 2 * h + low
                arrived(tok.at[v, place(2 - h, from_z)], ag_recv.at[v, 2 - h, from_z])
                arrived(tok.at[v, place(3, from_z)], ag_recv.at[v, 3, from_z])
        own_copy[v].wait()

    send_z(0)
    for v in range(WAVES):
        send_xy(v, own_block[v], z)
    for c in own_copy + loads[:3]:
        c.start()
    for c in loads[3:]:
        c.wait()

    def turn_tiles(first, last):
        @pl.loop(first, last)
        def _(i):
            gate_up_t[i] = gate_up[i].reshape(256, cols).T

    count = routes.shape[1]
    diagonal = lax.broadcasted_iota(jnp.int32, (count, count), 0) == lax.broadcasted_iota(
        jnp.int32, (count, count), 1
    )

    def as_column(row):
        return jnp.sum(jnp.where(diagonal, jnp.broadcast_to(row, (count, count)), 0.0), 1, keepdims=True)

    lane = lax.broadcasted_iota(jnp.int32, (8, 128), 1).astype(jnp.float32)
    packed = jnp.zeros((8, 128), jnp.float32)
    for k in range(routes.shape[0]):
        chosen = as_column(routes[k : k + 1, :].astype(jnp.float32))
        amount = as_column(weights[k : k + 1, :])
        for g in range(count // 8):
            packed += jnp.where(lane == chosen[8 * g : 8 * g + 8] + 16.0 * g, amount[8 * g : 8 * g + 8], 0.0)
    coef[0, z] = packed
    for k in (1, 2, 3):
        send(coef.at[0, z], coef.at[0, z], cf_send.at[k], cf_recv.at[z], z_peer(k))

    for c in loads[:2]:
        c.wait()
    turn_tiles(0, 3)
    pass_column(0)
    send_z(1)
    turn_tiles(3, 6)
    pass_diagonal(0)
    turn_tiles(6, 8)
    pass_column(1)
    send_z(2)
    for k in (1, 2, 3):
        from_z = (z + k) % 4
        arrived(coef.at[0, from_z], cf_recv.at[from_z])
    send(coef.at[0], coef.at[1], cf_send.at[4], cf_recv.at[4], x_peer)
    send(coef.at[0], coef.at[2], cf_send.at[5], cf_recv.at[5], y_peer)
    turn_tiles(8, tiles)

    def add_tile(v, i):
        x = tok[v].reshape(2 * half_rows, cols)
        sums = lax.dot_general(x, gate_up_t[i], NN, preferred_element_type=jnp.float32)
        gsend[v, i] = sums.astype(jnp.bfloat16).reshape(2, half_rows, 256)
        copy(gsend.at[v, i, 1 - n], grecv.at[v, i], g_send.at[v, i], g_recv.at[v, i], w, 1 - n).start()

    def hide_tile(v, i):
        arrived(grecv.at[v, i], g_recv.at[v, i])
        sums = gsend[v, i, n].astype(jnp.float32) + grecv[v, i].astype(jnp.float32)
        gate, up = sums[:, :128], sums[:, 128:]
        lanes = pl.ds(pl.multiple_of(i * 128, 128), 128)
        hid[v, n, :, lanes] = (gate / (1.0 + jnp.exp(-gate)) * up).astype(jnp.bfloat16)
        there = hid.at[v, n, :, lanes]
        copy(there, there, h_send.at[v, i], h_recv.at[v, i], w, 1 - n).start()

    def hidden_units(v, first, second, third):
        @pl.loop(0, LAG)
        def _(i):
            add_tile(v, i)

        first()

        @pl.loop(LAG, LAG + (tiles - LAG) // 2)
        def _(i):
            add_tile(v, i)
            hide_tile(v, i - LAG)

        second()

        @pl.loop(LAG + (tiles - LAG) // 2, tiles)
        def _(i):
            add_tile(v, i)
            hide_tile(v, i - LAG)

        third()

        @pl.loop(tiles - LAG, tiles)
        def _(i):
            hide_tile(v, i)

    def outputs(v, h):
        column = scale[v, pl.ds(8 * h, 8)].reshape(half_rows, 128)[:, 0:1]

        @pl.loop(0, cols // 256)
        def _(i):
            lanes = pl.ds(pl.multiple_of(i * 256, 256), 256)
            acc = lax.dot_general(hid[v, h], down[:, lanes], NN, preferred_element_type=jnp.float32)
            part[v, pl.ds(8 * h, 8), :, lanes] = (acc * column).astype(jnp.bfloat16).reshape(8, rows, 256)

    def other_hidden(v):
        @pl.loop(0, tiles)
        def _(i):
            lanes = pl.ds(pl.multiple_of(i * 128, 128), 128)
            arrived(hid.at[v, 1 - n, :, lanes], h_recv.at[v, i])

    def send_half(v, h):
        peer = x_peer + h * (y_peer - x_peer)
        for low in (0, 1):
            at = 2 * h + low
            send(part.at[v, place(3, at)], back.at[v, 0, at], rs_send.at[v, 0, at], rs_recv.at[v, 0, at], peer)
        for low in (0, 1):
            at = 2 * h + low
            send(
                part.at[v, place(1 + h, at)], back.at[v, 1 + h, at],
                rs_send.at[v, 1 + h, at], rs_recv.at[v, 1 + h, at], peer,
            )

    def relay_sums(v):
        for low in (0, 1):
            for h in (0, 1):
                at = 2 * h + low
                arrived(back.at[v, 0, at], rs_recv.at[v, 0, at])
                mine = part[v, place(2 - h, at)].astype(jnp.float32)
                part[v, place(2 - h, at)] = (mine + back[v, 0, at].astype(jnp.float32)).astype(jnp.bfloat16)
                send(
                    part.at[v, place(2 - h, at)], back.at[v, 2 - h, at],
                    rs_send.at[v, 2 - h, at], rs_recv.at[v, 2 - h, at], y_peer if h == 0 else x_peer,
                )

    def column_sums(v):
        for k in (2, 1, 3, 0):
            at = (z + k) % 4
            arrived(back.at[v, 1, at], rs_recv.at[v, 1, at])
            arrived(back.at[v, 2, at], rs_recv.at[v, 2, at])
            total = part[v, place(0, at)].astype(jnp.float32)
            total += back[v, 1, at].astype(jnp.float32) + back[v, 2, at].astype(jnp.float32)
            if k == 0:
                zrecv[v, z] = total.astype(jnp.bfloat16)
            else:
                zsend[v, k] = total.astype(jnp.bfloat16)
                send(zsend.at[v, k], zrecv.at[v, z], z_send.at[v, k], z_recv.at[v, z], z_peer(k))

    def finish(v):
        for k in (1, 3, 2):
            at = (z + k) % 4
            arrived(zrecv.at[v, at], z_recv.at[v, at])
        total = zrecv[v, 0].astype(jnp.float32) + zrecv[v, 1].astype(jnp.float32)
        total += zrecv[v, 2].astype(jnp.float32) + zrecv[v, 3].astype(jnp.float32)
        out[pl.ds(v * rows, rows), :] = total.astype(jnp.bfloat16)

    def make_scale():
        arrived(coef.at[2], cf_recv.at[5])
        arrived(coef.at[3], cf_recv.at[6])
        lane = lax.broadcasted_iota(jnp.int32, (4, 8, 128), 2)
        for column in range(4):
            block = coef[column]
            for g in range(tokens.shape[0] // 8):
                mine = jnp.sum(jnp.where(lane == 16 * g + w, block, 0.0), 2, keepdims=True)
                mine = jnp.broadcast_to(mine, (4, 8, 128))
                for at in range(4):
                    scale[g * 8 // rows, place(column, at), g % (rows // 8)] = mine[at]

    def give(v):
        outputs(v, n)
        send_half(v, n)
        other_hidden(v)
        outputs(v, 1 - n)
        send_half(v, 1 - n)

    def coef_diagonal():
        arrived(coef.at[1], cf_recv.at[4])
        send(coef.at[1], coef.at[3], cf_send.at[6], cf_recv.at[6], y_peer)

    def first_0():
        pass_diagonal(1)
        pass_column(2)
        send_z(3)

    def nothing():
        pass

    gather_rest(0)
    hidden_units(0, first_0, coef_diagonal, lambda: pass_column(3))
    make_scale()
    loads[2].wait()
    give(0)

    gather_rest(1)
    hidden_units(1, lambda: pass_diagonal(2), lambda: relay_sums(0), lambda: pass_diagonal(3))
    give(1)

    gather_rest(2)
    hidden_units(2, lambda: relay_sums(1), lambda: column_sums(0), nothing)
    give(2)

    gather_rest(3)
    hidden_units(3, nothing, lambda: relay_sums(2), lambda: column_sums(1))
    give(3)

    column_sums(2)
    relay_sums(3)
    column_sums(3)
    for v in range(WAVES):
        finish(v)

    for c in sent:
        c.wait_send()
    for v in range(WAVES):

        @pl.loop(0, tiles)
        def _(i):
            lanes = pl.ds(pl.multiple_of(i * 128, 128), 128)
            there = hid.at[v, n, :, lanes]
            copy(gsend.at[v, i, 1 - n], grecv.at[v, i], g_send.at[v, i], g_recv.at[v, i], w, 1 - n).wait_send()
            copy(there, there, h_send.at[v, i], h_recv.at[v, i], w, 1 - n).wait_send()


def gather_plan(tokens, routes, route_weight, w_gate, w_up, w_down):
    count = tokens.shape[0]
    hidden, cols = w_gate.shape[1:]
    tiles = hidden // 128
    rows = count // WAVES
    half = 8 * rows
    bf16, f32 = jnp.bfloat16, jnp.float32
    dma = pltpu.SemaphoreType.DMA
    vmem = pl.BlockSpec(memory_space=pltpu.VMEM)
    anywhere = pl.BlockSpec(memory_space=pl.ANY)
    flops = 2 * 16 * count * hidden * cols * 3
    return pl.pallas_call(
        kernel,
        out_shape=jax.ShapeDtypeStruct((count, cols), bf16),
        in_specs=[anywhere] * 6,
        out_specs=vmem,
        scratch_shapes=[
            pltpu.VMEM((route_weight.shape[1], count), jnp.int32),
            pltpu.VMEM((route_weight.shape[1], count), f32),
            pltpu.VMEM((WAVES, 16, rows, cols), bf16),
            pltpu.VMEM((tiles, 2, 128, cols), bf16),
            pltpu.VMEM((tiles, cols, 256), bf16),
            pltpu.VMEM((hidden, cols), bf16),
            pltpu.VMEM((4, 4, 8, 128), f32),
            pltpu.VMEM((WAVES, 16, rows // 8, 8, 128), f32),
            pltpu.VMEM((WAVES, tiles, 2, half, 256), bf16),
            pltpu.VMEM((WAVES, tiles, half, 256), bf16),
            pltpu.VMEM((WAVES, 2, half, hidden), bf16),
            pltpu.VMEM((WAVES, 16, rows, cols), bf16),
            pltpu.VMEM((WAVES, 3, 4, rows, cols), bf16),
            pltpu.VMEM((WAVES, 4, rows, cols), bf16),
            pltpu.VMEM((WAVES, 4, rows, cols), bf16),
            dma((5,)), dma((WAVES,)),
            dma((WAVES, 4, 4)), dma((WAVES, 4, 4)),
            dma((7,)), dma((7,)),
            dma((WAVES, tiles)), dma((WAVES, tiles)),
            dma((WAVES, tiles)), dma((WAVES, tiles)),
            dma((WAVES, 3, 4)), dma((WAVES, 3, 4)),
            dma((WAVES, 4)), dma((WAVES, 4)),
        ],
        compiler_params=pltpu.CompilerParams(
            collective_id=0, has_side_effects=True, vmem_limit_bytes=64 * 1024 * 1024 - 128 * 1024
        ),
        cost_estimate=pl.CostEstimate(
            flops=flops, bytes_accessed=3 * hidden * cols * 2, transcendentals=8 * count * hidden
        ),
    )(
        tokens, routes.T, route_weight.T,
        w_gate.reshape(tiles, 128, cols), w_up.reshape(tiles, 128, cols), w_down[0],
    )


def solution(mesh):
    chips = mesh.shape["wide"] == 16 and mesh.shape["narrow"] == 2
    return jax.shard_map(
        gather_plan if chips else slots_plan,
        mesh=mesh,
        in_specs=(
            P("wide", None),
            P("wide", None),
            P("wide", None),
            P("wide", None, "narrow"),
            P("wide", None, "narrow"),
            P("wide", None, "narrow"),
        ),
        out_specs=P("wide", "narrow"),
        check_vma=False,
    )
```
